32 devices in a mesh: animal: 8 (over z, core), snp: 4 (over y, x).
Axes of the slice: x: 2, y: 2, z: 4, core: 2. Of those that a mesh axis runs over, the one named last changes fastest.
Arguments:
- genotypes: int32 [16384, 8192], P('animal', 'snp'), may hold values from 0 to 2730, as said below
- allele_frequency: float32 [49152], P('snp'), may hold values from 0.05 to 0.5
- family_size: int32 [128], P('animal'), may hold values from 40 to 128, as said below
- rel_family: int32 [128], P('animal'), may hold values from 0 to 127, as said below
- rel_count: int32 [128], P('animal'), may hold values from 8 to 128, as said below
- own_block: bfloat16 [128, 128, 128], P('animal'), may hold values from -0.5 to 3
- rel_block: bfloat16 [128, 128, 128], P('animal'), may hold values from -0.5 to 0.5
- prior_solution: bfloat16 [16384, 128], P('animal'), may hold values from -6 to 6
- right_side: float32 [16384, 128], P('animal'), may hold values from -6 to 6
- step_scale: float32 [16384], P('animal'), may hold values from 0.1 to 0.3
Outputs:
- solution: float32 [16384, 128], P(('animal', 'snp'))
- residual: float32 [16384, 128], P(('animal', 'snp'))
The draws below stay inside these ranges and needn't reach their ends.
Inputs may be any that keep to these rules, and one draw needn't show every extreme that they name: `genotypes`: bits 2k and 2k + 1 of word w of a row hold the code 0, 1 or 2 of marker 6w + k, for k = 0 to 5; higher bits are zero; some word has all six codes 0 and some word all six codes 2. `family_size`: some family has all 128 slots live. `rel_family`: family f's relative family lies in the same block of 16 consecutive families as f or in one of the 3 blocks before it, and in the block exactly 3 before it for some family of every block that has one. `rel_count`: some family takes all 128 rows.
All inputs are finite; a program needn't handle non-finite values.
Results may differ from the reference program's by a relative error of at most 0.007.
Values may be sent and summed in bfloat16 or wider, within the bound.
No kernel may reach another device: no remote copies, remote signals or barrier semaphores. Data moves between devices by JAX's collectives and lax.ppermute only.
A program may use at most 256 MiB of HBM per device.

```python
import math
import jax
import jax.numpy as jnp
from jax import lax

FAMSIZE = 128
SNPS = 49152
COLS = 128
ITERS = 2
RSPAN = 3
KIN_SPAN_UNIT = 16
FAMILIES = 128
ROWS = 16384


def variant_millesimal(key):
    return jax.random.randint(jax.random.fold_in(key, 11), (SNPS,), 50, 501)


def draw_allele_frequency(key, part):
    return variant_millesimal(key).astype(jnp.float32) / 1000.0


def draw_genotypes(key, part):
    millesimal_scale = variant_millesimal(key)
    twin_copy_indicator = millesimal_scale * millesimal_scale
    bears_variant_indicator = twin_copy_indicator + 2 * millesimal_scale * (1000 - millesimal_scale)
    code_key = jax.random.fold_in(key, 12)

    def one_family(family_index):
        flat_random_draws = jax.random.randint(jax.random.fold_in(code_key, family_index), (FAMSIZE, SNPS), 0, 1000000)
        dosage_states = (flat_random_draws < bears_variant_indicator[None, :]).astype(jnp.int32) + (flat_random_draws < twin_copy_indicator[None, :]).astype(jnp.int32)
        grouped = dosage_states.reshape(FAMSIZE, SNPS // 6, 6)
        packed = jnp.zeros((FAMSIZE, SNPS // 6), jnp.int32)
        for position in range(6):
            packed = jnp.bitwise_or(packed, jnp.left_shift(grouped[:, :, position], jnp.int32(2 * position)))
        return packed
    blocks = lax.map(one_family, jnp.arange(FAMILIES, dtype=jnp.int32))
    words = blocks.reshape(ROWS, SNPS // 6)
    low_row = jax.random.randint(jax.random.fold_in(key, 13), (), 0, ROWS)
    low_col = jax.random.randint(jax.random.fold_in(key, 14), (), 0, SNPS // 6)
    high_row = jax.random.randint(jax.random.fold_in(key, 15), (), 0, ROWS)
    high_col = jax.random.randint(jax.random.fold_in(key, 16), (), 0, SNPS // 6)
    high_col = jnp.where((high_row == low_row) & (high_col == low_col), (low_col + 1) % (SNPS // 6), high_col)
    words = words.at[low_row, low_col].set(jnp.int32(0))
    words = words.at[high_row, high_col].set(jnp.int32(2730))
    return words


def draw_family_size(key, part):
    sizes = jax.random.randint(jax.random.fold_in(key, 21), (FAMILIES,), FAMSIZE * 5 // 16, FAMSIZE + 1)
    full_family = jax.random.randint(jax.random.fold_in(key, 22), (), 0, FAMILIES)
    return sizes.at[full_family].set(FAMSIZE).astype(jnp.int32)


def draw_rel_family(key, part):
    family_index = jnp.arange(FAMILIES, dtype=jnp.int32)
    device_index = family_index // KIN_SPAN_UNIT
    distance = jax.random.randint(jax.random.fold_in(key, 31), (FAMILIES,), 0, RSPAN + 1)
    chosen = jax.random.randint(jax.random.fold_in(key, 32), (FAMILIES // KIN_SPAN_UNIT,), 0, KIN_SPAN_UNIT)
    distance = jnp.where(family_index % KIN_SPAN_UNIT == chosen[device_index], RSPAN, distance)
    distance = jnp.minimum(distance, device_index)
    within = jax.random.randint(jax.random.fold_in(key, 33), (FAMILIES,), 0, KIN_SPAN_UNIT)
    return ((device_index - distance) * KIN_SPAN_UNIT + within).astype(jnp.int32)


def draw_rel_count(key, part):
    counts = jax.random.randint(jax.random.fold_in(key, 35), (FAMILIES,), FAMSIZE // 16, FAMSIZE + 1)
    full_family = jax.random.randint(jax.random.fold_in(key, 36), (), 0, FAMILIES)
    return counts.at[full_family].set(FAMSIZE).astype(jnp.int32)


def draw_own_block(key, part):
    noise = jax.random.normal(jax.random.fold_in(key, 41), (FAMILIES, FAMSIZE, FAMSIZE), jnp.float32)
    diagonal = jax.random.uniform(jax.random.fold_in(key, 42), (FAMILIES, FAMSIZE), jnp.float32, 1.5, 2.5)
    identity = jnp.eye(FAMSIZE, dtype=jnp.float32)
    offdiag = noise * (0.5 / math.sqrt(FAMSIZE)) * (1.0 - identity)[None, :, :]
    return (offdiag + identity[None, :, :] * diagonal[:, None, :]).astype(jnp.bfloat16)


def levels(key, dims, split, least, high):
    factor_of, own = 1.0, jax.random.fold_in(key, 6)
    for dim, parts in split:
        draws = jnp.exp(jax.random.uniform(jax.random.fold_in(own, dim), (parts,), jnp.float32, least / len(split), high / len(split)))
        factor_of = factor_of * jnp.repeat(draws, dims[dim] // parts).reshape([-1 if axis == dim else 1 for axis in range(len(dims))])
    return factor_of


def scatter_about(rng, shape, spread, reach, split=(), kind=jnp.bfloat16):
    level = levels(rng, shape, split, -0.22, 0.18) if split else 1.0
    array = jax.random.normal(rng, shape, jnp.float32) * spread * level
    return jnp.minimum(jnp.maximum(array, -reach), reach).astype(kind)


def setup_inputs(seed: int = 0) -> dict:
    streams_of = jax.random.split(jax.random.key(seed), 11)
    return {
        "genotypes": draw_genotypes(jax.random.fold_in(streams_of[10], 71), 0),
        "allele_frequency": draw_allele_frequency(jax.random.fold_in(streams_of[10], 71), 0),
        "family_size": draw_family_size(jax.random.fold_in(streams_of[10], 71), 0),
        "rel_family": draw_rel_family(jax.random.fold_in(streams_of[10], 71), 0),
        "rel_count": draw_rel_count(jax.random.fold_in(streams_of[10], 71), 0),
        "own_block": draw_own_block(jax.random.fold_in(streams_of[10], 71), 0),
        "rel_block": scatter_about(streams_of[6], (FAMILIES, FAMSIZE, FAMSIZE), FAMSIZE ** -0.5, 0.5, ((0, 8),)),
        "prior_solution": scatter_about(streams_of[7], (ROWS, COLS), 1.0, 6.0, ((0, 8),)),
        "right_side": scatter_about(streams_of[8], (ROWS, COLS), 1.0, 6.0, ((0, 8),), jnp.float32),
        "step_scale": jnp.clip(jnp.exp(math.log(0.3) - 1.0986123 * jax.random.uniform(streams_of[9], (ROWS,), jnp.float32) ** levels(streams_of[9], (ROWS,), ((0, 8),), -0.2, 0.2)), 0.1, 0.3),
    }


GEN_WEIGHT = 6.0


def decode_rows(genotypes, allele_frequency, live_rows):
    bit_shifts = 2 * jnp.arange(6, dtype=jnp.int32)
    dosage_states = jnp.bitwise_and(jnp.right_shift(genotypes[:, :, None], bit_shifts[None, None, :]), 3)
    dosage_states = dosage_states.reshape(genotypes.shape[0], genotypes.shape[1] * 6).astype(jnp.float32)
    centered = (dosage_states - 2.0 * allele_frequency[None, :]) * live_rows[:, None]
    return centered.astype(jnp.bfloat16)


def reference(genotypes, allele_frequency, family_size, rel_family, rel_count, own_block, rel_block, prior_solution, right_side, step_scale):
    slot_index = jnp.arange(FAMSIZE, dtype=jnp.int32)
    live_rows = (slot_index[None, :] < family_size[:, None]).astype(jnp.float32).reshape(-1)
    packed_blocks = genotypes.reshape(FAMILIES, FAMSIZE, SNPS // 6)
    live_blocks = live_rows.reshape(FAMILIES, FAMSIZE)
    keep_rows = slot_index[None, :, None] < rel_count[:, None, None]
    solution_now = live_rows[:, None] * prior_solution.astype(jnp.float32)
    residual = jnp.zeros((ROWS, COLS), jnp.float32)
    for iteration in range(ITERS):
        solution_half = solution_now.astype(jnp.bfloat16)
        half_blocks = solution_half.reshape(FAMILIES, FAMSIZE, COLS)

        def add_block(running, inputs):
            packed, live_part, half_part = inputs
            centered = decode_rows(packed, allele_frequency, live_part)
            product = lax.dot_general(centered, half_part, (((0,), (0,)), ((), ())), preferred_element_type=jnp.float32)
            return running + product, 0

        snp_sum = lax.scan(add_block, jnp.zeros((SNPS, COLS), jnp.float32), (packed_blocks, live_blocks, half_blocks))[0]
        snp_half = snp_sum.astype(jnp.bfloat16)

        def genomic_block(inputs):
            packed, live_part = inputs
            return jnp.dot(decode_rows(packed, allele_frequency, live_part), snp_half, preferred_element_type=jnp.float32)

        genomic = lax.map(genomic_block, (packed_blocks, live_blocks)).reshape(ROWS, COLS)
        family_half = solution_half.reshape(FAMILIES, FAMSIZE, COLS)
        relatives = jnp.where(keep_rows, family_half[rel_family], jnp.zeros_like(family_half))
        pedigree = jnp.einsum("fij,fjk->fik", own_block.astype(jnp.float32), family_half.astype(jnp.float32))
        pedigree = pedigree + jnp.einsum("fij,fjk->fik", rel_block.astype(jnp.float32), relatives.astype(jnp.float32))
        pedigree = pedigree.reshape(ROWS, COLS)
        residual = live_rows[:, None] * (right_side - solution_now - (GEN_WEIGHT / SNPS) * genomic - pedigree)
        solution_now = solution_now + step_scale[:, None] * residual
    return solution_now, residual
```

```python
import jax
import jax.numpy as jnp
from jax import lax
from jax.experimental import pallas as pl
from jax.experimental.pallas import tpu as pltpu
from jax.sharding import PartitionSpec as P

ITERS = 2
RSPAN = 3
GEN_WEIGHT = 6.0
CODES_PER_WORD = 6
CHUNKS = 8
CHAINS = 2

F8 = jnp.float8_e4m3fn
BF16 = jnp.bfloat16
F32 = jnp.float32
FINE = 16.0
TOP = 256.0
KERNEL_VMEM = 28 << 20

IN_VMEM = pl.BlockSpec(memory_space=pltpu.VMEM)
IN_SMEM = pl.BlockSpec(memory_space=pltpu.SMEM)


def in_vmem(array):
    return pltpu.with_memory_space_constraint(array, pltpu.VMEM)


def params():
    return pltpu.CompilerParams(vmem_limit_bytes=KERNEL_VMEM)


def dot(a, b, a_dim, b_dim):
    return lax.dot_general(a, b, (((a_dim,), (b_dim,)), ((), ())), preferred_element_type=F32)


def pieces(x):
    first = x.astype(BF16)
    left = x - first.astype(F32)
    second = left.astype(BF16)
    third = (left - second.astype(F32)).astype(BF16)
    return first, second, third


def two_parts(x):
    top = jnp.maximum(jnp.max(jnp.abs(x), axis=0, keepdims=True), 1e-30)
    y = x * (TOP / top)
    hi = y.astype(F8)
    lo = ((y - hi.astype(F32)) * FINE).astype(F8)
    return hi, lo, top * (1.0 / TOP)


def joined(product):
    half = product.shape[1] // 2
    return product[:, :half] + product[:, half:] * (1.0 / FINE)


class Order:
    def __init__(self):
        self.last = None

    def after(self, *arrays):
        if self.last is None:
            return arrays if len(arrays) > 1 else arrays[0]
        held = lax.optimization_barrier((*arrays, self.last))[:-1]
        return held if len(arrays) > 1 else held[0]

    def done(self, array):
        self.last = array
        return array


def centre_rows(minus_twice):
    width = minus_twice.shape[1]

    def body(p_ref, out_ref):
        a, b, c = pieces(p_ref[...])
        none = jnp.zeros((2, width), BF16)
        out_ref[...] = jnp.concatenate([a, a, a, b, b, c, none], axis=0)

    return pl.pallas_call(
        body,
        in_specs=[IN_VMEM],
        out_specs=IN_VMEM,
        out_shape=jax.ShapeDtypeStruct((8, width), BF16),
        compiler_params=params(),
        name="centre_rows",
    )(minus_twice)


def split_half(shares, slot):
    count = len(shares)
    share_rows, columns = shares[0].shape
    rows = count * share_rows

    def body(slot_ref, *refs):
        ins, (cat_ref, inv_ref, sums_ref, full_ref) = refs[:count], refs[count:]
        for k in range(count):
            at = pl.multiple_of(slot_ref[k] * share_rows, share_rows)
            full_ref[pl.ds(at, share_rows), :] = ins[k][...]
        hi, lo, inv = two_parts(full_ref[...].astype(F32))
        cat_ref[:, :columns] = hi
        cat_ref[:, columns:] = lo
        inv_ref[...] = jnp.broadcast_to(inv, (8, columns))
        total = jnp.sum(hi.astype(F32) + lo.astype(F32) * (1.0 / FINE), axis=0, keepdims=True) * inv
        a, b, c = pieces(total)
        none = jnp.zeros((2, columns), BF16)
        sums_ref[...] = jnp.concatenate([a, b, c, a, b, a, none], axis=0)

    return pl.pallas_call(
        body,
        in_specs=[IN_SMEM] + [IN_VMEM] * count,
        out_specs=(IN_VMEM,) * 3,
        out_shape=(
            pltpu.VMEM((rows, 2 * columns), F8),
            pltpu.VMEM((8, columns), F32),
            pltpu.VMEM((8, columns), BF16),
        ),
        scratch_shapes=[pltpu.VMEM((rows, columns), BF16)],
        compiler_params=params(),
        name="split_half",
    )(slot, *shares)


def marker_sums(codes, cat, inv, sums, centre):
    product = joined(dot(codes, cat, 0, 0)) * inv[0:1, :]
    return (product + dot(centre, sums, 0, 0)).astype(BF16)


def decode_and_sum(words, cat, inv, sums, centre, chunk, width):
    rows = words.shape[0]
    columns = inv.shape[1]
    markers = CODES_PER_WORD * width

    def body(words_ref, cat_ref, inv_ref, sums_ref, centre_ref, codes_ref, out_ref):
        for k in range(CODES_PER_WORD):
            code = jnp.bitwise_and(jnp.right_shift(words_ref[...], 2 * k), 3)
            codes_ref[:, k * width : (k + 1) * width] = code.astype(F32).astype(F8)
        out_ref[...] = marker_sums(
            codes_ref[...], cat_ref[...], inv_ref[...], sums_ref[...], centre_ref[...]
        )

    return pl.pallas_call(
        body,
        grid=(1,),
        in_specs=[
            pl.BlockSpec((rows, width), lambda i: (0, chunk)),
            IN_VMEM,
            IN_VMEM,
            IN_VMEM,
            pl.BlockSpec((8, markers), lambda i: (0, chunk)),
        ],
        out_specs=(IN_VMEM, IN_VMEM),
        out_shape=(pltpu.VMEM((rows, markers), F8), pltpu.VMEM((markers, columns), BF16)),
        compiler_params=params(),
        name="decode_and_sum",
    )(
        pltpu.with_memory_space_constraint(words, pltpu.HBM),
        in_vmem(cat),
        in_vmem(inv),
        in_vmem(sums),
        centre,
    )


def sum_again(codes, cat, inv, sums, centre, chunk):
    columns = inv.shape[1]
    markers = codes.shape[1]

    def body(codes_ref, cat_ref, inv_ref, sums_ref, centre_ref, out_ref):
        out_ref[...] = marker_sums(
            codes_ref[...], cat_ref[...], inv_ref[...], sums_ref[...], centre_ref[...]
        )

    return pl.pallas_call(
        body,
        grid=(1,),
        in_specs=[IN_VMEM] * 4 + [pl.BlockSpec((8, markers), lambda i: (0, chunk))],
        out_specs=IN_VMEM,
        out_shape=pltpu.VMEM((markers, columns), BF16),
        compiler_params=params(),
        name="sum_again",
    )(in_vmem(codes), in_vmem(cat), in_vmem(inv), in_vmem(sums), centre)


def add_genomic(codes, own, passed, other, centre, chunk, weight, running):
    markers = codes.shape[1]
    rows, columns = running.shape

    def body(codes_ref, own_ref, passed_ref, other_ref, centre_ref, run_ref, out_ref):
        total = own_ref[...].astype(F32) + passed_ref[...].astype(F32) + other_ref[...].astype(F32)
        hi, lo, inv = two_parts(total)
        cat = jnp.concatenate([hi, lo], axis=1)
        centre_part = dot(centre_ref[...], cat.astype(BF16), 1, 0)
        shift = centre_part[0:1, :] + centre_part[3:4, :] + centre_part[5:6, :]
        product = dot(codes_ref[...], cat, 1, 0) + shift
        out_ref[...] = run_ref[...] + joined(product) * (inv * weight)

    return pl.pallas_call(
        body,
        grid=(1,),
        in_specs=[IN_VMEM] * 4 + [pl.BlockSpec((8, markers), lambda i: (0, chunk)), IN_VMEM],
        out_specs=IN_VMEM,
        out_shape=pltpu.VMEM((rows, columns), F32),
        input_output_aliases={5: 0},
        compiler_params=params(),
        name="add_genomic",
    )(in_vmem(codes), in_vmem(own), in_vmem(passed), in_vmem(other), centre, in_vmem(running))


def pedigree(held, position, count, rel_block, own_part, own_half, base):
    families, order, _ = rel_block.shape
    share = own_part.shape[0]
    columns = own_half.shape[1]

    def body(pos_ref, count_ref, held_ref, rel_ref, own_ref, half_ref, base_ref, out_ref, rest_ref):
        row = lax.broadcasted_iota(jnp.int32, (order, columns), 0)
        for f in range(families):
            at = pl.multiple_of(pos_ref[f] * order, order)
            relative = held_ref[pl.ds(at, order), :]
            relative = jnp.where(row < count_ref[f], relative, jnp.zeros_like(relative))
            out_ref[f * order : (f + 1) * order, :] = dot(rel_ref[f], relative, 1, 0)
        for f in range(share):
            part = slice(f * order, (f + 1) * order)
            rest_ref[part, :] = base_ref[part, :] - dot(own_ref[f], half_ref[part, :], 1, 0)

    return pl.pallas_call(
        body,
        in_specs=[IN_SMEM, IN_SMEM] + [IN_VMEM] * 5,
        out_specs=(IN_VMEM, IN_VMEM),
        out_shape=(
            pltpu.VMEM((families * order, columns), F32),
            pltpu.VMEM((share * order, columns), F32),
        ),
        compiler_params=params(),
        name="pedigree",
    )(position, count, held, rel_block, own_part, own_half, base)


def by_distance(distance, arrays):
    result = None
    for d, array in enumerate(arrays):
        if array is None:
            continue
        result = array if result is None else jnp.where(distance == d, array, result)
    return result


def per_device(
    genotypes,
    allele_frequency,
    family_size,
    rel_family,
    rel_count,
    own_block,
    rel_block,
    prior_solution,
    right_side,
    step_scale,
):
    families, order, _ = own_block.shape
    rows, columns = prior_solution.shape
    words = genotypes.shape[1]
    animals = lax.axis_size("animal")
    snps = lax.axis_size("snp")
    device = lax.axis_index("animal")
    slot = lax.axis_index("snp")
    chips = animals // 2
    chip = device // 2
    core = device % 2
    distance = jnp.where(core == 0, chip, chips - 1 - chip)
    chunks = CHUNKS
    per_chain = chunks // CHAINS
    width = words // chunks
    weight = GEN_WEIGHT / (words * CODES_PER_WORD * snps)
    share = families // snps
    share_rows = share * order

    swap = [(i, i ^ 1) for i in range(animals)]
    along = [(i, i + 2) for i in range(0, animals - 2, 2)]
    along += [(i, i - 2) for i in range(3, animals, 2)]

    def mine(array, size):
        return lax.dynamic_slice_in_dim(array, slot * size, size, 0)

    live = (jnp.arange(order, dtype=jnp.int32)[None, :] < family_size[:, None]).reshape(rows, 1)
    live_part = mine(live.astype(F32), share_rows)
    right_part = mine(right_side, share_rows)
    scale_part = mine(step_scale, share_rows)[:, None]
    own_part = mine(own_block, share)
    half = jnp.where(live, prior_solution, jnp.zeros_like(prior_solution))
    own_half = mine(half, share_rows)
    solution_part = own_half.astype(F32)

    minus_twice = -2.0 * allele_frequency.reshape(chunks, width, CODES_PER_WORD)
    centre = centre_rows(minus_twice.transpose(0, 2, 1).reshape(1, -1))

    away = device - rel_family // families
    inside = rel_family % families
    position = jnp.clip(away * share + inside % share, 0, (RSPAN + 1) * share - 1)
    count = jnp.where(inside // share == slot, rel_count, 0)

    def held_rows(own_half):
        second = lax.ppermute(own_half, "animal", [(i, i + 2) for i in range(animals - 2)])
        third = lax.ppermute(own_half, "animal", [(i, i + 3) for i in range(1, animals - 3, 2)])
        sibling = lax.ppermute(own_half, "animal", swap)
        sibling_second = lax.ppermute(second, "animal", swap)
        even = core == 0
        return jnp.concatenate(
            [
                own_half,
                jnp.where(even, sibling_second, sibling),
                second,
                jnp.where(even, third, sibling_second),
            ],
            axis=0,
        )

    residual = None
    codes = [None] * chunks
    shares, places = [half], jnp.zeros((1,), jnp.int32)
    for iteration in range(ITERS):
        steps = Order()
        held = held_rows(own_half)
        cat, inv, sums = split_half(shares, places)
        steps.done(cat)

        sent, got, total = [None] * chunks, [None] * chunks, [None] * chunks
        running = rest = None

        def first_product(c):
            if iteration == 0:
                codes[c], sent[c] = decode_and_sum(
                    genotypes, steps.after(cat), inv, sums, centre, c, width
                )
            else:
                sent[c] = sum_again(codes[c], steps.after(cat), inv, sums, centre, c)
            steps.done(sent[c])
            got[c] = lax.ppermute(sent[c], "animal", swap)

        def chip_sum(c):
            total[c] = steps.done(
                (sent[c].astype(F32) + steps.after(got[c]).astype(F32)).astype(BF16)
            )

        received = [[] for _ in range(CHAINS)]
        passed, other = [None] * chunks, [None] * chunks
        waiting = []

        def second_product():
            nonlocal running
            c = waiting.pop(0)
            running = steps.done(
                add_genomic(
                    codes[c], total[c], passed[c], steps.after(other[c]), centre, c, weight, running
                )
            )

        for c in range(CHAINS):
            first_product(c)
        ready = CHAINS
        slots = per_chain + chips - 2
        for j in range(slots + 1):
            for chain in range(CHAINS):
                if j < per_chain:
                    chip_sum(j * CHAINS + chain)
                arrived = None
                if j > 0:
                    arrived = steps.after(received[chain][j - 1])
                    received[chain][j - 1] = arrived
                if j < slots:
                    options = [
                        total[(j - d) * CHAINS + chain] if 0 <= j - d < per_chain else None
                        for d in range(chips - 1)
                    ]
                    out = by_distance(distance, options)
                    if arrived is not None:
                        out = steps.done((out.astype(F32) + arrived.astype(F32)).astype(BF16))
                    received[chain].append(lax.ppermute(out, "animal", along))
                k = j - (chips - 1)
                if k >= 0:
                    c = k * CHAINS + chain
                    options = [received[chain][k + max(d - 1, 0)] for d in range(chips)]
                    passed[c] = steps.done(by_distance(distance, options))
                    other[c] = lax.ppermute(passed[c], "animal", swap)
                    waiting.append(c)
                if ready < chunks:
                    first_product(ready)
                    ready += 1
                if running is None and j == 1:
                    running, rest = pedigree(
                        steps.after(held),
                        position,
                        count,
                        rel_block,
                        own_part,
                        own_half,
                        right_part - solution_part,
                    )
                    steps.done(running)
                if len(waiting) > 1:
                    second_product()
        while waiting:
            second_product()

        parts = rest - mine(running, share_rows)
        for k in range(snps - 1, 0, -1):
            there = lax.dynamic_slice_in_dim(running, (slot ^ k) * share_rows, share_rows, 0)
            parts = parts - lax.ppermute(
                there.astype(BF16), "snp", [(i, i ^ k) for i in range(snps)]
            ).astype(F32)
        residual = live_part * parts
        solution_part = solution_part + scale_part * residual
        if iteration + 1 < ITERS:
            own_half = solution_part.astype(BF16)
            shares = [own_half] + [
                lax.ppermute(own_half, "snp", [(i, i ^ k) for i in range(snps)])
                for k in range(1, snps)
            ]
            places = jnp.stack([slot ^ k for k in range(snps)]).astype(jnp.int32)
    return solution_part, residual


def solution(mesh):
    in_specs = (
        P("animal", "snp"),
        P("snp"),
        P("animal"),
        P("animal"),
        P("animal"),
        P("animal", None, None),
        P("animal", None, None),
        P("animal", None),
        P("animal", None),
        P("animal"),
    )
    out_specs = (P(("animal", "snp"), None), P(("animal", "snp"), None))
    return jax.shard_map(
        per_device, mesh=mesh, in_specs=in_specs, out_specs=out_specs, check_vma=False
    )
```

```python
import jax
import jax.numpy as jnp
from jax import lax
from jax.experimental import pallas as pl
from jax.experimental.pallas import tpu as pltpu
from jax.sharding import PartitionSpec as P

ITERS = 2
RSPAN = 3
GEN_WEIGHT = 6.0
CODES_PER_WORD = 6
CHUNKS = 8
CHAINS = 2
LANES = 128
PIECE_ROWS = 16
FETCHES = 1
BANDS = 2

F8 = jnp.float8_e4m3fn
BF16 = jnp.bfloat16
F32 = jnp.float32
FINE = 16.0
TOP = 256.0
KERNEL_VMEM = 16 << 20

IN_VMEM = pl.BlockSpec(memory_space=pltpu.VMEM)
IN_SMEM = pl.BlockSpec(memory_space=pltpu.SMEM)


def in_vmem(array):
    return pltpu.with_memory_space_constraint(array, pltpu.VMEM)


def params():
    return pltpu.CompilerParams(vmem_limit_bytes=KERNEL_VMEM)


def cost():
    return pl.CostEstimate(flops=0, bytes_accessed=0, transcendentals=0)


def dot(a, b, a_dim, b_dim):
    return lax.dot_general(a, b, (((a_dim,), (b_dim,)), ((), ())), preferred_element_type=F32)


def pieces(x):
    first = x.astype(BF16)
    left = x - first.astype(F32)
    second = left.astype(BF16)
    third = (left - second.astype(F32)).astype(BF16)
    return first, second, third


def two_parts(x):
    top = jnp.max(jnp.abs(x), axis=0, keepdims=True)
    scale = jnp.ones_like(top)
    inverse = jnp.ones_like(top)
    for power in (64, 32, 16, 8, 4, 2, 1):
        up, down = 2.0**power, 2.0**-power
        low = top < TOP * down
        high = top >= TOP * up * 0.5
        step = jnp.where(low, up, jnp.where(high, down, 1.0))
        back = jnp.where(low, down, jnp.where(high, up, 1.0))
        top, scale, inverse = top * step, scale * step, inverse * back
    y = x * scale
    hi = y.astype(F8)
    lo = ((y - hi.astype(F32)) * FINE).astype(F8)
    return hi, lo, inverse


def joined(product):
    half = product.shape[1] // 2
    return product[:, :half] + product[:, half:] * (1.0 / FINE)


class Order:
    def __init__(self):
        self.last = None

    def after(self, *arrays):
        if self.last is None:
            return arrays if len(arrays) > 1 else arrays[0]
        held = lax.optimization_barrier((*arrays, self.last))[:-1]
        return held if len(arrays) > 1 else held[0]

    def done(self, array):
        self.last = array
        return array


def fetch_words(all_ref, words_ref, arrived, chunk):
    rows, width = words_ref.shape
    band = rows // FETCHES
    return [
        pltpu.make_async_copy(
            all_ref.at[pl.ds(i * band, band), pl.ds(chunk * width, width)],
            words_ref.at[pl.ds(i * band, band), :],
            arrived.at[i],
        )
        for i in range(FETCHES)
    ]


def write_half(half, cat_ref, inv_ref, sums_ref):
    columns = half.shape[1]
    hi, lo, inv = two_parts(half.astype(F32))
    cat_ref[:, :columns] = hi
    cat_ref[:, columns:] = lo
    inv_ref[...] = jnp.broadcast_to(inv, inv_ref.shape)
    total = jnp.sum(hi.astype(F32) + lo.astype(F32) * (1.0 / FINE), axis=0, keepdims=True) * inv
    a, b, c = pieces(total)
    none = jnp.zeros((PIECE_ROWS - 6, columns), BF16)
    sums_ref[...] = jnp.concatenate([a, b, c, a, b, a, none], axis=0)


def half_shapes(rows, columns):
    return [
        pltpu.VMEM((rows, 2 * columns), F8),
        pltpu.VMEM((8, columns), F32),
        pltpu.VMEM((PIECE_ROWS, columns), BF16),
    ]


def begin(genotypes, frequency, family_size, prior, width):
    rows, columns = prior.shape
    families = family_size.shape[0]
    order = rows // families
    words = genotypes.shape[1]
    lines = words // LANES
    per_chunk = width // LANES
    span = CODES_PER_WORD * LANES

    def body(
        all_ref, freq_ref, size_ref, prior_ref, half_ref, cat_ref, inv_ref, sums_ref, centre_ref, words_ref, arrived
    ):
        fetches = fetch_words(all_ref, words_ref, arrived, 0)
        for fetch in fetches:
            fetch.start()
        row = lax.broadcasted_iota(jnp.int32, (order, columns), 0)
        for f in range(families):
            part = slice(f * order, (f + 1) * order)
            block = prior_ref[part, :]
            half_ref[part, :] = jnp.where(row < size_ref[f], block, jnp.zeros_like(block))
        write_half(half_ref[...], cat_ref, inv_ref, sums_ref)

        a, b, c = pieces(-2.0 * freq_ref[...])
        which = lax.broadcasted_iota(jnp.int32, (lines * PIECE_ROWS, span), 0) % PIECE_ROWS
        picked = jnp.where(
            which < 3,
            a.astype(F32),
            jnp.where(which < 5, b.astype(F32), jnp.where(which < 6, c.astype(F32), 0.0)),
        ).astype(BF16)
        source = lax.broadcasted_iota(jnp.int32, (span, LANES), 0)
        lane = lax.broadcasted_iota(jnp.int32, (span, LANES), 1)
        code_of = source - CODES_PER_WORD * lane
        for k in range(CODES_PER_WORD):
            place = jnp.where(code_of == k, 1.0, 0.0).astype(BF16)
            moved = dot(picked, place, 1, 0).astype(BF16)
            for line in range(lines):
                chunk, inner = divmod(line, per_chunk)
                at = (chunk * CODES_PER_WORD + k) * width + inner * LANES
                centre_ref[:, at : at + LANES] = moved[line * PIECE_ROWS : (line + 1) * PIECE_ROWS, :]
        for fetch in fetches:
            fetch.wait()

    return pl.pallas_call(
        body,
        in_specs=[pl.BlockSpec(memory_space=pl.ANY), IN_VMEM, IN_SMEM, IN_VMEM],
        out_specs=[IN_VMEM] * 6,
        out_shape=[
            pltpu.VMEM((rows, columns), BF16),
            *half_shapes(rows, columns),
            pltpu.VMEM((PIECE_ROWS, words * CODES_PER_WORD), BF16),
            pltpu.VMEM((rows, width), genotypes.dtype),
        ],
        scratch_shapes=[pltpu.SemaphoreType.DMA((FETCHES,))],
        compiler_params=params(),
        cost_estimate=cost(),
        name="begin",
    )(pltpu.with_memory_space_constraint(genotypes, pltpu.HBM), frequency, family_size, prior)


def split_half(shares, slot):
    count = len(shares)
    share_rows, columns = shares[0].shape
    rows = count * share_rows

    def body(slot_ref, *refs):
        ins, (cat_ref, inv_ref, sums_ref, full_ref) = refs[:count], refs[count:]
        for k in range(count):
            at = pl.multiple_of(slot_ref[k] * share_rows, share_rows)
            full_ref[pl.ds(at, share_rows), :] = ins[k][...]
        write_half(full_ref[...], cat_ref, inv_ref, sums_ref)

    return pl.pallas_call(
        body,
        in_specs=[IN_SMEM] + [IN_VMEM] * count,
        out_specs=[IN_VMEM] * 3,
        out_shape=half_shapes(rows, columns),
        scratch_shapes=[pltpu.VMEM((rows, columns), BF16)],
        compiler_params=params(),
        cost_estimate=cost(),
        name="split_half",
    )(slot, *shares)


def marker_sums(codes, cat, inv, sums, centre):
    product = joined(dot(codes, cat, 0, 0)) * inv[0:1, :]
    return (product + dot(centre, sums, 0, 0)).astype(BF16)


def decode_and_sum(genotypes, words, cat, inv, sums, centre, chunk, chunks):
    rows, width = words.shape
    columns = inv.shape[1]
    markers = CODES_PER_WORD * width
    more = chunk + 1 < chunks

    band = rows // BANDS

    def body(all_ref, words_ref, cat_ref, inv_ref, sums_ref, centre_ref, kept_ref, out_ref, *rest):
        *rest, codes_ref, stored = rest
        copies = fetch_words(all_ref, *rest, chunk + 1) if more else []
        for copy in copies:
            copy.start()
        for b in range(BANDS):
            part = pl.ds(b * band, band)
            for k in range(CODES_PER_WORD):
                code = jnp.bitwise_and(jnp.right_shift(words_ref[part, :], 2 * k), 3)
                codes_ref[part, k * width : (k + 1) * width] = code.astype(F32).astype(F8)
            copy = pltpu.make_async_copy(codes_ref.at[part, :], kept_ref.at[part, :], stored.at[b])
            copy.start()
            copies.append(copy)
        out_ref[...] = marker_sums(
            codes_ref[...],
            cat_ref[...],
            inv_ref[...],
            sums_ref[...],
            centre_ref[:, chunk * markers : (chunk + 1) * markers],
        )
        for copy in copies:
            copy.wait()

    out_shape = [pltpu.HBM((rows, markers), F8), pltpu.VMEM((markers, columns), BF16)]
    scratch = [pltpu.VMEM((rows, markers), F8), pltpu.SemaphoreType.DMA((BANDS,))]
    if more:
        out_shape.append(pltpu.VMEM((rows, width), words.dtype))
        scratch = [pltpu.SemaphoreType.DMA((FETCHES,)), *scratch]
    return pl.pallas_call(
        body,
        in_specs=[pl.BlockSpec(memory_space=pl.ANY)] + [IN_VMEM] * 5,
        out_specs=[pl.BlockSpec(memory_space=pl.ANY)] + [IN_VMEM] * (len(out_shape) - 1),
        out_shape=out_shape,
        scratch_shapes=scratch,
        compiler_params=params(),
        cost_estimate=cost(),
        name="decode_and_sum",
    )(
        pltpu.with_memory_space_constraint(genotypes, pltpu.HBM),
        *map(in_vmem, (words, cat, inv, sums, centre)),
    )


def sum_again(codes, cat, inv, sums, centre, chunk):
    columns = inv.shape[1]
    markers = codes.shape[1]

    def body(codes_ref, cat_ref, inv_ref, sums_ref, centre_ref, out_ref):
        out_ref[...] = marker_sums(
            codes_ref[...],
            cat_ref[...],
            inv_ref[...],
            sums_ref[...],
            centre_ref[:, chunk * markers : (chunk + 1) * markers],
        )

    return pl.pallas_call(
        body,
        in_specs=[IN_VMEM] * 5,
        out_specs=IN_VMEM,
        out_shape=pltpu.VMEM((markers, columns), BF16),
        compiler_params=params(),
        cost_estimate=cost(),
        name="sum_again",
    )(*map(in_vmem, (codes, cat, inv, sums, centre)))


def genomic_step(codes_ref, own_ref, passed_ref, other_ref, centre_ref, chunk, weight):
    markers = codes_ref.shape[1]
    total = own_ref[...].astype(F32) + passed_ref[...].astype(F32) + other_ref[...].astype(F32)
    hi, lo, inv = two_parts(total)
    cat = jnp.concatenate([hi, lo], axis=1)
    centre = centre_ref[:, chunk * markers : (chunk + 1) * markers]
    centre_part = dot(centre, cat.astype(BF16), 1, 0)
    shift = centre_part[0:1, :] + centre_part[3:4, :] + centre_part[5:6, :]
    product = dot(codes_ref[...], cat, 1, 0) + shift
    return joined(product) * (inv * weight)


def add_genomic(codes, own, passed, other, centre, chunk, weight, running):
    rows, columns = running.shape

    def body(codes_ref, own_ref, passed_ref, other_ref, centre_ref, run_ref, out_ref):
        out_ref[...] = run_ref[...] + genomic_step(
            codes_ref, own_ref, passed_ref, other_ref, centre_ref, chunk, weight
        )

    return pl.pallas_call(
        body,
        in_specs=[IN_VMEM] * 6,
        out_specs=IN_VMEM,
        out_shape=pltpu.VMEM((rows, columns), F32),
        input_output_aliases={5: 0},
        compiler_params=params(),
        cost_estimate=cost(),
        name="add_genomic",
    )(*map(in_vmem, (codes, own, passed, other, centre, running)))


def last_genomic(codes, own, passed, other, centre, chunk, weight, running, rest, slots):
    columns = running.shape[1]
    share_rows = rest.shape[0]
    count = slots.shape[0]

    def body(slot_ref, codes_ref, own_ref, passed_ref, other_ref, centre_ref, run_ref, rest_ref, *refs):
        outs, all_ref = refs[:count], refs[count]
        all_ref[...] = run_ref[...] + genomic_step(
            codes_ref, own_ref, passed_ref, other_ref, centre_ref, chunk, weight
        )
        for k in range(count):
            at = pl.multiple_of(slot_ref[k] * share_rows, share_rows)
            part = all_ref[pl.ds(at, share_rows), :]
            outs[k][...] = rest_ref[...] - part if k == 0 else part.astype(BF16)

    return pl.pallas_call(
        body,
        in_specs=[IN_SMEM] + [IN_VMEM] * 7,
        out_specs=[IN_VMEM] * count,
        out_shape=[
            pltpu.VMEM((share_rows, columns), F32 if k == 0 else BF16) for k in range(count)
        ],
        scratch_shapes=[pltpu.VMEM(running.shape, F32)],
        compiler_params=params(),
        cost_estimate=cost(),
        name="last_genomic",
    )(slots, *map(in_vmem, (codes, own, passed, other, centre, running, rest)))


def pedigree(held, position, count, rel_block, own_part, right_part, solution_part):
    families, order, _ = rel_block.shape
    share = own_part.shape[0]
    own_half = held[0]
    share_rows, columns = own_half.shape

    def body(pos_ref, count_ref, *refs):
        held_refs, refs = refs[: len(held)], refs[len(held) :]
        rel_ref, own_ref, right_ref, solution_ref, out_ref, rest_ref, all_ref = refs
        for d, ref in enumerate(held_refs):
            all_ref[d * share_rows : (d + 1) * share_rows, :] = ref[...]
        row = lax.broadcasted_iota(jnp.int32, (order, columns), 0)
        for f in range(families):
            at = pl.multiple_of(pos_ref[f] * order, order)
            relative = all_ref[pl.ds(at, order), :]
            relative = jnp.where(row < count_ref[f], relative, jnp.zeros_like(relative))
            out_ref[f * order : (f + 1) * order, :] = dot(rel_ref[f], relative, 1, 0)
        for f in range(share):
            part = slice(f * order, (f + 1) * order)
            own = dot(own_ref[f], held_refs[0][part, :], 1, 0)
            rest_ref[part, :] = right_ref[part, :] - solution_ref[part, :] - own

    return pl.pallas_call(
        body,
        in_specs=[IN_SMEM, IN_SMEM] + [IN_VMEM] * (len(held) + 4),
        out_specs=(IN_VMEM, IN_VMEM),
        out_shape=(
            pltpu.VMEM((families * order, columns), F32),
            pltpu.VMEM((share * order, columns), F32),
        ),
        scratch_shapes=[pltpu.VMEM((len(held) * share_rows, columns), own_half.dtype)],
        compiler_params=params(),
        cost_estimate=cost(),
        name="pedigree",
    )(position, count, *held, rel_block, own_part, right_part, solution_part)


def by_distance(distance, arrays):
    result = None
    for d, array in enumerate(arrays):
        if array is None:
            continue
        result = array if result is None else jnp.where(distance == d, array, result)
    return result


def per_device(
    genotypes,
    allele_frequency,
    family_size,
    rel_family,
    rel_count,
    own_block,
    rel_block,
    prior_solution,
    right_side,
    step_scale,
):
    families, order, _ = own_block.shape
    rows, columns = prior_solution.shape
    words = genotypes.shape[1]
    animals = lax.axis_size("animal")
    snps = lax.axis_size("snp")
    device = lax.axis_index("animal")
    slot = lax.axis_index("snp")
    chips = animals // 2
    chip = device // 2
    core = device % 2
    distance = jnp.where(core == 0, chip, chips - 1 - chip)
    chunks = CHUNKS
    per_chain = chunks // CHAINS
    width = words // chunks
    weight = GEN_WEIGHT / (words * CODES_PER_WORD * snps)
    share = families // snps
    share_rows = share * order

    swap = [(i, i ^ 1) for i in range(animals)]
    along = [(i, i + 2) for i in range(0, animals - 2, 2)] + [(animals - 2, animals - 1)]
    along += [(i, i - 2) for i in range(3, animals, 2)] + [(1, 0)]
    two_up = [(i, i + 2) for i in range(animals - 2)]
    crossed = {i: i + 3 for i in range(1, animals - 3, 2)}
    crossed.update({b: a for a, b in list(crossed.items())})
    three_up = [(i, crossed.get(i, i)) for i in range(animals)]

    def mine(array, size):
        return lax.dynamic_slice_in_dim(array, slot * size, size, 0)

    places = jnp.stack([slot ^ k for k in range(snps)]).astype(jnp.int32)
    frequency = jnp.repeat(
        allele_frequency.reshape(words // LANES, CODES_PER_WORD * LANES), PIECE_ROWS, axis=0
    )
    half, cat, inv, sums, centre, first_words = begin(
        genotypes, frequency, family_size, prior_solution, width
    )
    own_half = mine(half, share_rows)
    right_part = mine(right_side, share_rows)
    scale_part = mine(step_scale, share_rows)[:, None]
    own_part = mine(own_block, share)
    sizes = mine(family_size, share)
    live_part = (jnp.arange(order, dtype=jnp.int32)[None, :] < sizes[:, None]).reshape(-1, 1)
    solution_part = own_half.astype(F32)

    away = device - rel_family // families
    inside = rel_family % families
    position = jnp.clip(away * share + inside % share, 0, (RSPAN + 1) * share - 1)
    count = jnp.where(inside // share == slot, rel_count, 0)

    residual = None
    codes = [None] * chunks
    fetched = [first_words]
    for iteration in range(ITERS):
        steps = Order()
        if iteration > 0:
            cat, inv, sums = split_half(shares, places)
        steps.done(cat)

        sent, got, total = [None] * chunks, [None] * chunks, [None] * chunks
        running = rest = None

        def first_product(c):
            nonlocal fetched
            if iteration == 0:
                codes[c], sent[c], *fetched = decode_and_sum(
                    genotypes, fetched[0], steps.after(cat), inv, sums, centre, c, chunks
                )
            else:
                sent[c] = sum_again(codes[c], steps.after(cat), inv, sums, centre, c)
            steps.done(sent[c])
            got[c] = lax.ppermute(sent[c], "animal", swap)

        def chip_sum(c):
            total[c] = steps.done(
                (sent[c].astype(F32) + steps.after(got[c]).astype(F32)).astype(BF16)
            )

        received = [[] for _ in range(CHAINS)]
        passed, other = [None] * chunks, [None] * chunks
        waiting = []

        def chunk_of(c):
            return codes[c], total[c], passed[c], steps.after(other[c]), centre, c, weight, running

        def second_product():
            nonlocal running
            running = steps.done(add_genomic(*chunk_of(waiting.pop(0))))

        for c in range(CHAINS):
            first_product(c)
        ready = CHAINS
        slots = per_chain + chips - 2
        for j in range(slots + 1):
            for chain in range(CHAINS):
                if j < per_chain:
                    chip_sum(j * CHAINS + chain)
                arrived = None
                if j > 0:
                    arrived = steps.after(received[chain][j - 1])
                    received[chain][j - 1] = arrived
                if j < slots:
                    options = [
                        total[(j - d) * CHAINS + chain] if 0 <= j - d < per_chain else None
                        for d in range(chips - 1)
                    ]
                    out = by_distance(distance, options)
                    if arrived is not None:
                        both = (out.astype(F32) + arrived.astype(F32)).astype(BF16)
                        out = steps.done(jnp.where(distance == 0, out, both))
                    received[chain].append(lax.ppermute(out, "animal", along))
                k = j - (chips - 1)
                if k >= 0:
                    c = k * CHAINS + chain
                    options = [received[chain][k + max(d - 1, 0)] for d in range(chips)]
                    options = steps.after(*options)
                    nothing = jnp.zeros_like(options[0])
                    passed[c] = steps.done(by_distance(distance, [nothing, *options[1:]]))
                    other[c] = lax.ppermute(passed[c], "animal", swap)
                    waiting.append(c)
                if ready < chunks:
                    first_product(ready)
                    ready += 1
                at = j * CHAINS + chain
                if at == 1:
                    second = lax.ppermute(steps.after(own_half), "animal", two_up)
                elif at == 2:
                    third = lax.ppermute(steps.after(own_half, second)[0], "animal", three_up)
                elif at == 3:
                    sibling = lax.ppermute(steps.after(own_half, third)[0], "animal", swap)
                elif at == 4:
                    sibling_second = lax.ppermute(steps.after(second, sibling)[0], "animal", swap)
                elif at == 5:
                    even = core == 0
                    held = [
                        own_half,
                        jnp.where(even, sibling_second, sibling),
                        second,
                        jnp.where(even, third, sibling_second),
                    ]
                    held[1] = steps.after(held[1])
                    running, rest = pedigree(
                        held, position, count, rel_block, own_part, right_part, solution_part
                    )
                    steps.done(running)
                if len(waiting) > 1:
                    second_product()
        while len(waiting) > 1:
            second_product()
        parts, *there = last_genomic(*chunk_of(waiting.pop(0)), rest, places)
        for k in range(snps - 1, 0, -1):
            here = lax.ppermute(there[k - 1], "snp", [(i, i ^ k) for i in range(snps)])
            parts = parts - here.astype(F32)
        residual = jnp.where(live_part, parts, 0.0)
        solution_part = solution_part + scale_part * residual
        if iteration + 1 < ITERS:
            own_half = solution_part.astype(BF16)
            shares = [own_half] + [
                lax.ppermute(own_half, "snp", [(i, i ^ k) for i in range(snps)])
                for k in range(1, snps)
            ]
    return solution_part, residual


def solution(mesh):
    in_specs = (
        P("animal", "snp"),
        P("snp"),
        P("animal"),
        P("animal"),
        P("animal"),
        P("animal", None, None),
        P("animal", None, None),
        P("animal", None),
        P("animal", None),
        P("animal"),
    )
    out_specs = (P(("animal", "snp"), None), P(("animal", "snp"), None))
    return jax.shard_map(
        per_device, mesh=mesh, in_specs=in_specs, out_specs=out_specs, check_vma=False
    )
```

```python
import jax
import jax.numpy as jnp
from jax import lax
from jax.experimental import pallas as pl
from jax.experimental.pallas import tpu as pltpu
from jax.sharding import PartitionSpec as P

ITERS = 2
RSPAN = 3
GEN_WEIGHT = 6.0
CODES_PER_WORD = 6
CHUNKS = 8
CHAINS = 2
LANES = 128
PIECE_ROWS = 16
FETCHES = 1
STORES = 2
ROW_BANDS = 8

F8 = jnp.float8_e5m2
BF16 = jnp.bfloat16
F32 = jnp.float32
KERNEL_VMEM = 10 << 20

IN_VMEM = pl.BlockSpec(memory_space=pltpu.VMEM)
IN_SMEM = pl.BlockSpec(memory_space=pltpu.SMEM)


def in_vmem(array):
    return pltpu.with_memory_space_constraint(array, pltpu.VMEM)


def params():
    return pltpu.CompilerParams(vmem_limit_bytes=KERNEL_VMEM)


def cost():
    return pl.CostEstimate(flops=0, bytes_accessed=0, transcendentals=0)


def dot(a, b, a_dim, b_dim):
    return lax.dot_general(a, b, (((a_dim,), (b_dim,)), ((), ())), preferred_element_type=F32)


def pieces(x):
    first = x.astype(BF16)
    left = x - first.astype(F32)
    second = left.astype(BF16)
    third = (left - second.astype(F32)).astype(BF16)
    return first, second, third


class Order:
    def __init__(self):
        self.last = None

    def after(self, *arrays):
        if self.last is None:
            return arrays if len(arrays) > 1 else arrays[0]
        held = lax.optimization_barrier((*arrays, self.last))[:-1]
        return held if len(arrays) > 1 else held[0]

    def done(self, array):
        self.last = array
        return array


def fetch_words(all_ref, words_ref, arrived, chunk):
    rows, width = words_ref.shape
    band = rows // FETCHES
    return [
        pltpu.make_async_copy(
            all_ref.at[pl.ds(i * band, band), pl.ds(chunk * width, width)],
            words_ref.at[pl.ds(i * band, band), :],
            arrived.at[i],
        )
        for i in range(FETCHES)
    ]


def sum_rows(half):
    a, b, c = pieces(jnp.sum(half.astype(F32), axis=0, keepdims=True))
    none = jnp.zeros((PIECE_ROWS - 6, half.shape[1]), BF16)
    return jnp.concatenate([a, b, c, a, b, a, none], axis=0)


def begin(genotypes, frequency, family_size, prior, width):
    rows, columns = prior.shape
    families = family_size.shape[0]
    order = rows // families
    words = genotypes.shape[1]
    lines = words // LANES
    per_chunk = width // LANES
    span = CODES_PER_WORD * LANES

    def body(
        all_ref, freq_ref, size_ref, prior_ref, half_ref, sums_ref, centre_ref, words_ref, arrived
    ):
        fetches = fetch_words(all_ref, words_ref, arrived, 0)
        for fetch in fetches:
            fetch.start()
        row = lax.broadcasted_iota(jnp.int32, (order, columns), 0)
        for f in range(families):
            part = slice(f * order, (f + 1) * order)
            block = prior_ref[part, :]
            half_ref[part, :] = jnp.where(row < size_ref[f], block, jnp.zeros_like(block))
        sums_ref[...] = sum_rows(half_ref[...])

        a, b, c = pieces(-2.0 * freq_ref[...])
        which = lax.broadcasted_iota(jnp.int32, (lines * PIECE_ROWS, span), 0) % PIECE_ROWS
        picked = jnp.where(
            which < 3,
            a.astype(F32),
            jnp.where(which < 5, b.astype(F32), jnp.where(which < 6, c.astype(F32), 0.0)),
        ).astype(BF16)
        source = lax.broadcasted_iota(jnp.int32, (span, LANES), 0)
        lane = lax.broadcasted_iota(jnp.int32, (span, LANES), 1)
        code_of = source - CODES_PER_WORD * lane
        for k in range(CODES_PER_WORD):
            place = jnp.where(code_of == k, 1.0, 0.0).astype(BF16)
            moved = dot(picked, place, 1, 0).astype(BF16)
            for line in range(lines):
                chunk, inner = divmod(line, per_chunk)
                at = (chunk * CODES_PER_WORD + k) * width + inner * LANES
                centre_ref[:, at : at + LANES] = moved[line * PIECE_ROWS : (line + 1) * PIECE_ROWS, :]
        for fetch in fetches:
            fetch.wait()

    return pl.pallas_call(
        body,
        in_specs=[pl.BlockSpec(memory_space=pl.ANY), IN_VMEM, IN_SMEM, IN_VMEM],
        out_specs=[IN_VMEM] * 4,
        out_shape=[
            pltpu.VMEM((rows, columns), BF16),
            pltpu.VMEM((PIECE_ROWS, columns), BF16),
            pltpu.VMEM((PIECE_ROWS, words * CODES_PER_WORD), BF16),
            pltpu.VMEM((rows, width), genotypes.dtype),
        ],
        scratch_shapes=[pltpu.SemaphoreType.DMA((FETCHES,))],
        compiler_params=params(),
        cost_estimate=cost(),
        name="begin",
    )(pltpu.with_memory_space_constraint(genotypes, pltpu.HBM), frequency, family_size, prior)


def join_half(shares, slot):
    count = len(shares)
    share_rows, columns = shares[0].shape
    rows = count * share_rows

    def body(slot_ref, *refs):
        ins, (half_ref, sums_ref) = refs[:count], refs[count:]
        for k in range(count):
            at = pl.multiple_of(slot_ref[k] * share_rows, share_rows)
            half_ref[pl.ds(at, share_rows), :] = ins[k][...]
        sums_ref[...] = sum_rows(half_ref[...])

    return pl.pallas_call(
        body,
        in_specs=[IN_SMEM] + [IN_VMEM] * count,
        out_specs=[IN_VMEM] * 2,
        out_shape=[pltpu.VMEM((rows, columns), BF16), pltpu.VMEM((PIECE_ROWS, columns), BF16)],
        compiler_params=params(),
        cost_estimate=cost(),
        name="join_half",
    )(slot, *shares)


def marker_sums(codes, half, sums, centre, k):
    return (dot(codes, half, 0, 0) * 4.0**-k + dot(centre, sums, 0, 0)).astype(BF16)


def decode_and_sum(genotypes, words, half, sums, centre, chunk, chunks):
    rows, width = words.shape
    columns = half.shape[1]
    markers = CODES_PER_WORD * width
    more = chunk + 1 < chunks
    group = CODES_PER_WORD // STORES

    def body(all_ref, words_ref, half_ref, sums_ref, centre_ref, kept_ref, out_ref, *rest):
        *rest, codes_ref, stored = rest
        copies = fetch_words(all_ref, *rest, chunk + 1) if more else []
        for copy in copies:
            copy.start()
        for k in range(CODES_PER_WORD):
            here = slice(k * width, (k + 1) * width)
            codes_ref[:, here] = jnp.bitwise_and(words_ref[...], 3 << (2 * k)).astype(F32).astype(F8)
            out_ref[here, :] = marker_sums(
                codes_ref[:, here].astype(BF16),
                half_ref[...],
                sums_ref[...],
                centre_ref[:, chunk * markers + k * width : chunk * markers + (k + 1) * width],
                k,
            )
            if (k + 1) % group == 0:
                part = pl.ds((k + 1 - group) * width, group * width)
                copy = pltpu.make_async_copy(
                    codes_ref.at[:, part], kept_ref.at[:, part], stored.at[k // group]
                )
                copy.start()
                copies.append(copy)
        for copy in copies:
            copy.wait()

    out_shape = [pltpu.HBM((rows, markers), F8), pltpu.VMEM((markers, columns), BF16)]
    scratch = [pltpu.VMEM((rows, markers), F8), pltpu.SemaphoreType.DMA((STORES,))]
    if more:
        out_shape.append(pltpu.VMEM((rows, width), words.dtype))
        scratch = [pltpu.SemaphoreType.DMA((FETCHES,)), *scratch]
    return pl.pallas_call(
        body,
        in_specs=[pl.BlockSpec(memory_space=pl.ANY)] + [IN_VMEM] * 4,
        out_specs=[pl.BlockSpec(memory_space=pl.ANY)] + [IN_VMEM] * (len(out_shape) - 1),
        out_shape=out_shape,
        scratch_shapes=scratch,
        compiler_params=params(),
        cost_estimate=cost(),
        name="decode_and_sum",
    )(
        pltpu.with_memory_space_constraint(genotypes, pltpu.HBM),
        *map(in_vmem, (words, half, sums, centre)),
    )


def sum_again(codes, half, sums, centre, chunk):
    rows, markers = codes.shape
    columns = half.shape[1]
    width = markers // CODES_PER_WORD

    def body(codes_ref, half_ref, sums_ref, centre_ref, out_ref):
        for k in range(CODES_PER_WORD):
            here = slice(k * width, (k + 1) * width)
            out_ref[here, :] = marker_sums(
                codes_ref[:, here].astype(BF16),
                half_ref[...],
                sums_ref[...],
                centre_ref[:, chunk * markers + k * width : chunk * markers + (k + 1) * width],
                k,
            )

    return pl.pallas_call(
        body,
        in_specs=[IN_VMEM] * 4,
        out_specs=IN_VMEM,
        out_shape=pltpu.VMEM((markers, columns), BF16),
        compiler_params=params(),
        cost_estimate=cost(),
        name="sum_again",
    )(*map(in_vmem, (codes, half, sums, centre)))


def genomic_steps(codes_ref, own_ref, passed_ref, other_ref, centre_ref, chunk, weight):
    rows, markers = codes_ref.shape
    total = own_ref[...].astype(F32) + passed_ref[...].astype(F32) + other_ref[...].astype(F32)
    total = total.astype(BF16)
    centre = dot(centre_ref[:, chunk * markers : (chunk + 1) * markers], total, 1, 0)
    shift = centre[0:1, :] + centre[3:4, :] + centre[5:6, :]
    width = markers // CODES_PER_WORD
    scaled = jnp.concatenate(
        [total[k * width : (k + 1) * width, :] * BF16(4.0**-k) for k in range(CODES_PER_WORD)]
    )
    band = rows // ROW_BANDS
    for b in range(ROW_BANDS):
        here = slice(b * band, (b + 1) * band)
        yield here, (dot(codes_ref[here, :].astype(BF16), scaled, 1, 0) + shift) * weight


def add_genomic(codes, own, passed, other, centre, chunk, weight, running):
    rows, columns = running.shape

    def body(codes_ref, own_ref, passed_ref, other_ref, centre_ref, run_ref, out_ref):
        for here, step in genomic_steps(
            codes_ref, own_ref, passed_ref, other_ref, centre_ref, chunk, weight
        ):
            out_ref[here, :] = run_ref[here, :] + step

    return pl.pallas_call(
        body,
        in_specs=[IN_VMEM] * 6,
        out_specs=IN_VMEM,
        out_shape=pltpu.VMEM((rows, columns), F32),
        input_output_aliases={5: 0},
        compiler_params=params(),
        cost_estimate=cost(),
        name="add_genomic",
    )(*map(in_vmem, (codes, own, passed, other, centre, running)))


def last_genomic(codes, own, passed, other, centre, chunk, weight, running, rest, slots):
    columns = running.shape[1]
    share_rows = rest.shape[0]
    count = slots.shape[0]

    def body(slot_ref, codes_ref, own_ref, passed_ref, other_ref, centre_ref, run_ref, rest_ref, *refs):
        outs, all_ref = refs[:count], refs[count]
        for here, step in genomic_steps(
            codes_ref, own_ref, passed_ref, other_ref, centre_ref, chunk, weight
        ):
            all_ref[here, :] = run_ref[here, :] + step
        for k in range(count):
            at = pl.multiple_of(slot_ref[k] * share_rows, share_rows)
            part = all_ref[pl.ds(at, share_rows), :]
            outs[k][...] = rest_ref[...] - part if k == 0 else part.astype(BF16)

    return pl.pallas_call(
        body,
        in_specs=[IN_SMEM] + [IN_VMEM] * 7,
        out_specs=[IN_VMEM] * count,
        out_shape=[
            pltpu.VMEM((share_rows, columns), F32 if k == 0 else BF16) for k in range(count)
        ],
        scratch_shapes=[pltpu.VMEM(running.shape, F32)],
        compiler_params=params(),
        cost_estimate=cost(),
        name="last_genomic",
    )(slots, *map(in_vmem, (codes, own, passed, other, centre, running, rest)))


def pedigree(held, position, count, rel_block, own_part, right_part, solution_part):
    families, order, _ = rel_block.shape
    share = own_part.shape[0]
    own_half = held[0]
    share_rows, columns = own_half.shape

    def body(pos_ref, count_ref, *refs):
        held_refs, refs = refs[: len(held)], refs[len(held) :]
        rel_ref, own_ref, right_ref, solution_ref, out_ref, rest_ref, all_ref = refs
        for d, ref in enumerate(held_refs):
            all_ref[d * share_rows : (d + 1) * share_rows, :] = ref[...]
        row = lax.broadcasted_iota(jnp.int32, (order, columns), 0)
        for f in range(families):
            at = pl.multiple_of(pos_ref[f] * order, order)
            relative = all_ref[pl.ds(at, order), :]
            relative = jnp.where(row < count_ref[f], relative, jnp.zeros_like(relative))
            out_ref[f * order : (f + 1) * order, :] = dot(rel_ref[f], relative, 1, 0)
        for f in range(share):
            part = slice(f * order, (f + 1) * order)
            own = dot(own_ref[f], held_refs[0][part, :], 1, 0)
            rest_ref[part, :] = right_ref[part, :] - solution_ref[part, :] - own

    return pl.pallas_call(
        body,
        in_specs=[IN_SMEM, IN_SMEM] + [IN_VMEM] * (len(held) + 4),
        out_specs=(IN_VMEM, IN_VMEM),
        out_shape=(
            pltpu.VMEM((families * order, columns), F32),
            pltpu.VMEM((share * order, columns), F32),
        ),
        scratch_shapes=[pltpu.VMEM((len(held) * share_rows, columns), own_half.dtype)],
        compiler_params=params(),
        cost_estimate=cost(),
        name="pedigree",
    )(position, count, *held, rel_block, own_part, right_part, solution_part)


def by_distance(distance, arrays):
    result = None
    for d, array in enumerate(arrays):
        if array is None:
            continue
        result = array if result is None else jnp.where(distance == d, array, result)
    return result


def per_device(
    genotypes,
    allele_frequency,
    family_size,
    rel_family,
    rel_count,
    own_block,
    rel_block,
    prior_solution,
    right_side,
    step_scale,
):
    families, order, _ = own_block.shape
    rows, columns = prior_solution.shape
    words = genotypes.shape[1]
    animals = lax.axis_size("animal")
    snps = lax.axis_size("snp")
    device = lax.axis_index("animal")
    slot = lax.axis_index("snp")
    chips = animals // 2
    chip = device // 2
    core = device % 2
    distance = jnp.where(core == 0, chip, chips - 1 - chip)
    chunks = CHUNKS
    per_chain = chunks // CHAINS
    width = words // chunks
    markers = width * CODES_PER_WORD
    weight = GEN_WEIGHT / (words * CODES_PER_WORD * snps)
    share = families // snps
    share_rows = share * order

    swap = [(i, i ^ 1) for i in range(animals)]
    along = [(i, i + 2) for i in range(0, animals - 2, 2)] + [(animals - 2, animals - 1)]
    along += [(i, i - 2) for i in range(3, animals, 2)] + [(1, 0)]
    def mine(array, size):
        return lax.dynamic_slice_in_dim(array, slot * size, size, 0)

    places = jnp.stack([slot ^ k for k in range(snps)]).astype(jnp.int32)
    frequency = jnp.repeat(
        allele_frequency.reshape(words // LANES, CODES_PER_WORD * LANES), PIECE_ROWS, axis=0
    )
    half, sums, centre, first_words = begin(
        genotypes, frequency, family_size, prior_solution, width
    )
    own_half = mine(half, share_rows)
    right_part = mine(right_side, share_rows)
    scale_part = mine(step_scale, share_rows)[:, None]
    own_part = mine(own_block, share)
    sizes = mine(family_size, share)
    live_part = (jnp.arange(order, dtype=jnp.int32)[None, :] < sizes[:, None]).reshape(-1, 1)
    solution_part = own_half.astype(F32)

    away = device - rel_family // families
    inside = rel_family % families
    position = jnp.clip(away * share + inside % share, 0, (RSPAN + 1) * share - 1)
    count = jnp.where(inside // share == slot, rel_count, 0)

    residual = None
    codes = [None] * chunks
    fetched = [first_words]
    for iteration in range(ITERS):
        steps = Order()
        sibling = lax.ppermute(own_half, "animal", swap)
        if iteration > 0:
            *shares, sibling = lax.optimization_barrier((*shares, sibling))
            half, sums = join_half(shares, places)
        steps.done(half)

        sent, got, total = [None] * chunks, [None] * chunks, [None] * chunks
        running = rest = None

        def first_product(c):
            nonlocal fetched
            if iteration == 0:
                codes[c], sent[c], *fetched = decode_and_sum(
                    genotypes, fetched[0], steps.after(half), sums, centre, c, chunks
                )
            else:
                sent[c] = sum_again(codes[c], steps.after(half), sums, centre, c)
            steps.done(sent[c])
            got[c] = lax.ppermute(sent[c], "animal", swap)

        def chip_sum(c):
            total[c] = steps.done(
                (sent[c].astype(F32) + steps.after(got[c]).astype(F32)).astype(BF16)
            )

        received = [[] for _ in range(CHAINS)]
        passed, other = [None] * chunks, [None] * chunks
        waiting = []

        def chunk_of(c):
            return codes[c], total[c], passed[c], steps.after(other[c]), centre, c, weight, running

        def second_product():
            nonlocal running
            running = steps.done(add_genomic(*chunk_of(waiting.pop(0))))

        for c in range(CHAINS):
            first_product(c)
        ready = CHAINS
        slots = per_chain + chips - 2
        for j in range(slots + 1):
            for chain in range(CHAINS):
                if j < per_chain:
                    chip_sum(j * CHAINS + chain)
                arrived = None
                if j > 0:
                    arrived = steps.after(received[chain][j - 1])
                    riders = arrived[markers:]
                    arrived = arrived[:markers]
                    received[chain][j - 1] = arrived
                if j < slots:
                    options = [
                        total[(j - d) * CHAINS + chain] if 0 <= j - d < per_chain else None
                        for d in range(chips - 1)
                    ]
                    out = by_distance(distance, options)
                    if arrived is not None:
                        both = (out.astype(F32) + arrived.astype(F32)).astype(BF16)
                        out = steps.done(jnp.where(distance == 0, out, both))
                    if chain == 0 and j < 2:
                        out = lax.optimization_barrier((out, out))[0]
                        rider = [own_half, sibling] if j == 0 else [riders[share_rows:]]
                        out = steps.done(jnp.concatenate([out, *rider], axis=0))
                    received[chain].append(lax.ppermute(out, "animal", along))
                if chain == 0 and j == 1:
                    below = riders
                    across = lax.ppermute(below, "animal", swap)
                k = j - (chips - 1)
                if k >= 0:
                    c = k * CHAINS + chain
                    options = [received[chain][k + max(d - 1, 0)] for d in range(chips)]
                    options = steps.after(*options)
                    nothing = jnp.zeros_like(options[0])
                    passed[c] = steps.done(by_distance(distance, [nothing, *options[1:]]))
                    other[c] = lax.ppermute(passed[c], "animal", swap)
                    waiting.append(c)
                if ready < chunks:
                    first_product(ready)
                    ready += 1
                if chain == 0 and j == 2:
                    first, second = below[share_rows:], below[:share_rows]
                    held = [
                        own_half,
                        jnp.where(core == 0, first, sibling),
                        jnp.where(core == 0, second, across[share_rows:]),
                        jnp.where(core == 0, riders, across[:share_rows]),
                    ]
                    held[1] = steps.after(held[1])
                    running, rest = pedigree(
                        held, position, count, rel_block, own_part, right_part, solution_part
                    )
                    steps.done(running)
                if len(waiting) > 1:
                    second_product()
        while len(waiting) > 1:
            second_product()
        parts, *there = last_genomic(*chunk_of(waiting.pop(0)), rest, places)
        for k in range(snps - 1, 0, -1):
            here = lax.ppermute(there[k - 1], "snp", [(i, i ^ k) for i in range(snps)])
            parts = parts - here.astype(F32)
        residual = jnp.where(live_part, parts, 0.0)
        solution_part = solution_part + scale_part * residual
        if iteration + 1 < ITERS:
            own_half = solution_part.astype(BF16)
            shares = [own_half] + [
                lax.ppermute(own_half, "snp", [(i, i ^ k) for i in range(snps)])
                for k in range(1, snps)
            ]
    return solution_part, residual


def solution(mesh):
    in_specs = (
        P("animal", "snp"),
        P("snp"),
        P("animal"),
        P("animal"),
        P("animal"),
        P("animal", None, None),
        P("animal", None, None),
        P("animal", None),
        P("animal", None),
        P("animal"),
    )
    out_specs = (P(("animal", "snp"), None), P(("animal", "snp"), None))
    return jax.shard_map(
        per_device, mesh=mesh, in_specs=in_specs, out_specs=out_specs, check_vma=False
    )
```

```python
import jax
import jax.numpy as jnp
from jax import lax
from jax.experimental import pallas as pl
from jax.experimental.pallas import tpu as pltpu
from jax.sharding import PartitionSpec as P

ITERS = 2
RSPAN = 3
GEN_WEIGHT = 6.0
CODES_PER_WORD = 6
CHUNKS = 8
CHAINS = 2
LANES = 128
PIECE_ROWS = 16
FETCHES = 1
STORES = 2
ROW_BANDS = 8

F8 = jnp.float8_e5m2
BF16 = jnp.bfloat16
F32 = jnp.float32
KERNEL_VMEM = 10 << 20

IN_VMEM = pl.BlockSpec(memory_space=pltpu.VMEM)
IN_SMEM = pl.BlockSpec(memory_space=pltpu.SMEM)


def in_vmem(array):
    return pltpu.with_memory_space_constraint(array, pltpu.VMEM)


def params():
    return pltpu.CompilerParams(vmem_limit_bytes=KERNEL_VMEM)


def cost():
    return pl.CostEstimate(flops=0, bytes_accessed=0, transcendentals=0)


def dot(a, b, a_dim, b_dim):
    return lax.dot_general(a, b, (((a_dim,), (b_dim,)), ((), ())), preferred_element_type=F32)


def pieces(x):
    first = x.astype(BF16)
    left = x - first.astype(F32)
    second = left.astype(BF16)
    third = (left - second.astype(F32)).astype(BF16)
    return first, second, third


class Order:
    def __init__(self):
        self.last = None

    def after(self, *arrays):
        if self.last is None:
            return arrays if len(arrays) > 1 else arrays[0]
        held = lax.optimization_barrier((*arrays, self.last))[:-1]
        return held if len(arrays) > 1 else held[0]

    def done(self, array):
        self.last = array
        return array


def fetch_words(all_ref, words_ref, arrived, chunk):
    rows, width = words_ref.shape
    band = rows // FETCHES
    return [
        pltpu.make_async_copy(
            all_ref.at[pl.ds(i * band, band), pl.ds(chunk * width, width)],
            words_ref.at[pl.ds(i * band, band), :],
            arrived.at[i],
        )
        for i in range(FETCHES)
    ]


def sum_rows(half):
    a, b, c = pieces(jnp.sum(half.astype(F32), axis=0, keepdims=True))
    none = jnp.zeros((PIECE_ROWS - 6, half.shape[1]), BF16)
    return jnp.concatenate([a, b, c, a, b, a, none], axis=0)


def begin(genotypes, frequency, family_size, prior, width):
    rows, columns = prior.shape
    families = family_size.shape[0]
    order = rows // families
    words = genotypes.shape[1]
    lines = words // LANES
    per_chunk = width // LANES
    span = CODES_PER_WORD * LANES

    def body(
        all_ref,
        freq_ref,
        size_ref,
        prior_all,
        half_ref,
        sums_ref,
        centre_ref,
        words_ref,
        prior_ref,
        arrived,
        prior_arrived,
    ):
        prior_fetch = pltpu.make_async_copy(prior_all, prior_ref, prior_arrived)
        prior_fetch.start()
        fetches = fetch_words(all_ref, words_ref, arrived, 0)
        for fetch in fetches:
            fetch.start()

        lined = [
            jnp.broadcast_to(freq_ref[:, i * span : (i + 1) * span], (PIECE_ROWS, span)) for i in range(lines)
        ]
        a, b, c = pieces(-2.0 * jnp.concatenate(lined, axis=0))
        which = lax.broadcasted_iota(jnp.int32, (lines * PIECE_ROWS, span), 0) % PIECE_ROWS
        picked = jnp.where(
            which < 3,
            a.astype(F32),
            jnp.where(which < 5, b.astype(F32), jnp.where(which < 6, c.astype(F32), 0.0)),
        ).astype(BF16)
        source = lax.broadcasted_iota(jnp.int32, (span, LANES), 0)
        lane = lax.broadcasted_iota(jnp.int32, (span, LANES), 1)
        code_of = source - CODES_PER_WORD * lane
        for k in range(CODES_PER_WORD):
            place = jnp.where(code_of == k, 1.0, 0.0).astype(BF16)
            moved = dot(picked, place, 1, 0).astype(BF16)
            for line in range(lines):
                chunk, inner = divmod(line, per_chunk)
                at = (chunk * CODES_PER_WORD + k) * width + inner * LANES
                centre_ref[:, at : at + LANES] = moved[line * PIECE_ROWS : (line + 1) * PIECE_ROWS, :]
        prior_fetch.wait()
        row = lax.broadcasted_iota(jnp.int32, (order, columns), 0)
        for f in range(families):
            part = slice(f * order, (f + 1) * order)
            block = prior_ref[part, :]
            half_ref[part, :] = jnp.where(row < size_ref[f], block, jnp.zeros_like(block))
        sums_ref[...] = sum_rows(half_ref[...])
        for fetch in fetches:
            fetch.wait()

    return pl.pallas_call(
        body,
        in_specs=[pl.BlockSpec(memory_space=pl.ANY), IN_VMEM, IN_SMEM, pl.BlockSpec(memory_space=pl.ANY)],
        out_specs=[IN_VMEM] * 4,
        out_shape=[
            pltpu.VMEM((rows, columns), BF16),
            pltpu.VMEM((PIECE_ROWS, columns), BF16),
            pltpu.VMEM((PIECE_ROWS, words * CODES_PER_WORD), BF16),
            pltpu.VMEM((rows, width), genotypes.dtype),
        ],
        scratch_shapes=[
            pltpu.VMEM((rows, columns), prior.dtype),
            pltpu.SemaphoreType.DMA((FETCHES,)),
            pltpu.SemaphoreType.DMA,
        ],
        compiler_params=params(),
        cost_estimate=cost(),
        name="begin",
    )(
        pltpu.with_memory_space_constraint(genotypes, pltpu.HBM),
        frequency,
        family_size,
        pltpu.with_memory_space_constraint(prior, pltpu.HBM),
    )


def join_half(shares, slot):
    count = len(shares)
    share_rows, columns = shares[0].shape
    rows = count * share_rows

    def body(slot_ref, *refs):
        ins, (half_ref, sums_ref) = refs[:count], refs[count:]
        for k in range(count):
            at = pl.multiple_of(slot_ref[k] * share_rows, share_rows)
            half_ref[pl.ds(at, share_rows), :] = ins[k][...]
        sums_ref[...] = sum_rows(half_ref[...])

    return pl.pallas_call(
        body,
        in_specs=[IN_SMEM] + [IN_VMEM] * count,
        out_specs=[IN_VMEM] * 2,
        out_shape=[pltpu.VMEM((rows, columns), BF16), pltpu.VMEM((PIECE_ROWS, columns), BF16)],
        compiler_params=params(),
        cost_estimate=cost(),
        name="join_half",
    )(slot, *shares)


def marker_sums(codes, half, sums, centre, k):
    return (dot(codes, half, 0, 0) * 4.0**-k + dot(centre, sums, 0, 0)).astype(BF16)


def decode_and_sum(genotypes, words, half, sums, centre, chunk, chunks):
    rows, width = words.shape
    columns = half.shape[1]
    markers = CODES_PER_WORD * width
    more = chunk + 1 < chunks
    group = CODES_PER_WORD // STORES

    def body(all_ref, words_ref, half_ref, sums_ref, centre_ref, kept_ref, out_ref, *rest):
        *rest, codes_ref, stored = rest
        copies = fetch_words(all_ref, *rest, chunk + 1) if more else []
        for copy in copies:
            copy.start()
        for k in range(CODES_PER_WORD):
            here = slice(k * width, (k + 1) * width)
            codes_ref[:, here] = jnp.bitwise_and(words_ref[...], 3 << (2 * k)).astype(F32).astype(F8)
            out_ref[here, :] = marker_sums(
                codes_ref[:, here].astype(BF16),
                half_ref[...],
                sums_ref[...],
                centre_ref[:, chunk * markers + k * width : chunk * markers + (k + 1) * width],
                k,
            )
            if (k + 1) % group == 0:
                part = pl.ds((k + 1 - group) * width, group * width)
                copy = pltpu.make_async_copy(
                    codes_ref.at[:, part], kept_ref.at[:, part], stored.at[k // group]
                )
                copy.start()
                copies.append(copy)
        for copy in copies:
            copy.wait()

    out_shape = [pltpu.HBM((rows, markers), F8), pltpu.VMEM((markers, columns), BF16)]
    scratch = [pltpu.VMEM((rows, markers), F8), pltpu.SemaphoreType.DMA((STORES,))]
    if more:
        out_shape.append(pltpu.VMEM((rows, width), words.dtype))
        scratch = [pltpu.SemaphoreType.DMA((FETCHES,)), *scratch]
    return pl.pallas_call(
        body,
        in_specs=[pl.BlockSpec(memory_space=pl.ANY)] + [IN_VMEM] * 4,
        out_specs=[pl.BlockSpec(memory_space=pl.ANY)] + [IN_VMEM] * (len(out_shape) - 1),
        out_shape=out_shape,
        scratch_shapes=scratch,
        compiler_params=params(),
        cost_estimate=cost(),
        name="decode_and_sum",
    )(
        pltpu.with_memory_space_constraint(genotypes, pltpu.HBM),
        *map(in_vmem, (words, half, sums, centre)),
    )


def sum_again(codes, half, sums, centre, chunk):
    rows, markers = codes.shape
    columns = half.shape[1]
    width = markers // CODES_PER_WORD

    def body(codes_ref, half_ref, sums_ref, centre_ref, out_ref):
        for k in range(CODES_PER_WORD):
            here = slice(k * width, (k + 1) * width)
            out_ref[here, :] = marker_sums(
                codes_ref[:, here].astype(BF16),
                half_ref[...],
                sums_ref[...],
                centre_ref[:, chunk * markers + k * width : chunk * markers + (k + 1) * width],
                k,
            )

    return pl.pallas_call(
        body,
        in_specs=[IN_VMEM] * 4,
        out_specs=IN_VMEM,
        out_shape=pltpu.VMEM((markers, columns), BF16),
        compiler_params=params(),
        cost_estimate=cost(),
        name="sum_again",
    )(*map(in_vmem, (codes, half, sums, centre)))


def genomic_steps(codes_ref, own_ref, passed_ref, other_ref, centre_ref, chunk, weight):
    rows, markers = codes_ref.shape
    total = own_ref[...].astype(F32) + passed_ref[...].astype(F32) + other_ref[...].astype(F32)
    total = total.astype(BF16)
    centre = dot(centre_ref[:, chunk * markers : (chunk + 1) * markers], total, 1, 0)
    shift = centre[0:1, :] + centre[3:4, :] + centre[5:6, :]
    width = markers // CODES_PER_WORD
    scaled = jnp.concatenate(
        [total[k * width : (k + 1) * width, :] * BF16(4.0**-k) for k in range(CODES_PER_WORD)]
    )
    band = rows // ROW_BANDS
    for b in range(ROW_BANDS):
        here = slice(b * band, (b + 1) * band)
        yield here, (dot(codes_ref[here, :].astype(BF16), scaled, 1, 0) + shift) * weight


def add_genomic(codes, own, passed, other, centre, chunk, weight, running):
    rows, columns = running.shape

    def body(codes_ref, own_ref, passed_ref, other_ref, centre_ref, run_ref, out_ref):
        for here, step in genomic_steps(
            codes_ref, own_ref, passed_ref, other_ref, centre_ref, chunk, weight
        ):
            out_ref[here, :] = run_ref[here, :] + step

    return pl.pallas_call(
        body,
        in_specs=[IN_VMEM] * 6,
        out_specs=IN_VMEM,
        out_shape=pltpu.VMEM((rows, columns), F32),
        input_output_aliases={5: 0},
        compiler_params=params(),
        cost_estimate=cost(),
        name="add_genomic",
    )(*map(in_vmem, (codes, own, passed, other, centre, running)))


def last_genomic(codes, own, passed, other, centre, chunk, weight, running, rest, slots):
    rows, columns = running.shape
    share_rows = rest.shape[0]
    count = rows // share_rows

    def body(slot_ref, codes_ref, own_ref, passed_ref, other_ref, centre_ref, run_ref, rest_ref, *refs):
        outs, all_ref = refs[:count], refs[count]
        for here, step in genomic_steps(
            codes_ref, own_ref, passed_ref, other_ref, centre_ref, chunk, weight
        ):
            all_ref[here, :] = run_ref[here, :] + step
        for k in range(count):
            at = pl.multiple_of(slot_ref[k] * share_rows, share_rows)
            part = all_ref[pl.ds(at, share_rows), :]
            outs[k][...] = rest_ref[...] - part if k == 0 else part.astype(BF16)

    return pl.pallas_call(
        body,
        in_specs=[IN_SMEM] + [IN_VMEM] * 7,
        out_specs=[IN_VMEM] * count,
        out_shape=[
            pltpu.VMEM((share_rows, columns), F32 if k == 0 else BF16) for k in range(count)
        ],
        scratch_shapes=[pltpu.VMEM(running.shape, F32)],
        compiler_params=params(),
        cost_estimate=cost(),
        name="last_genomic",
    )(slots, *map(in_vmem, (codes, own, passed, other, centre, running, rest)))


def pedigree(held, rel_family, rel_count, places, rel_block, own_block, right_side, solution_part):
    families, order, _ = rel_block.shape
    own_half = held[0]
    share_rows, columns = own_half.shape
    share = share_rows // order

    def body(family_ref, count_ref, places_ref, *refs):
        held_refs, refs = refs[: len(held)], refs[len(held) :]
        rel_ref, solution_ref, own_all, right_all, out_ref, rest_ref, all_ref, own_ref, right_ref, arrived = refs
        slot, device = places_ref[0], places_ref[places_ref.shape[0] - 1]
        family = slot * share
        first = pl.multiple_of(places_ref[0] * share_rows, share_rows)
        fetches = [
            pltpu.make_async_copy(own_all.at[pl.ds(family, share)], own_ref, arrived.at[0]),
            pltpu.make_async_copy(right_all.at[pl.ds(first, share_rows), :], right_ref, arrived.at[1]),
        ]
        for fetch in fetches:
            fetch.start()
        for d, ref in enumerate(held_refs):
            all_ref[d * share_rows : (d + 1) * share_rows, :] = ref[...]
        row = lax.broadcasted_iota(jnp.int32, (order, columns), 0)
        for f in range(families):
            away = device - lax.div(family_ref[f], families)
            inside = lax.rem(family_ref[f], families)
            at = jnp.clip(away * share + lax.rem(inside, share), 0, len(held) * share - 1)
            count = jnp.where(lax.div(inside, share) == slot, count_ref[f], 0)
            relative = all_ref[pl.ds(pl.multiple_of(at * order, order), order), :]
            relative = jnp.where(row < count, relative, jnp.zeros_like(relative))
            out_ref[f * order : (f + 1) * order, :] = dot(rel_ref[f], relative, 1, 0)
        for fetch in fetches:
            fetch.wait()
        for f in range(share):
            part = slice(f * order, (f + 1) * order)
            own = dot(own_ref[f], held_refs[0][part, :], 1, 0)
            rest_ref[part, :] = right_ref[part, :] - solution_ref[part, :] - own

    return pl.pallas_call(
        body,
        in_specs=[IN_SMEM] * 3
        + [IN_VMEM] * (len(held) + 2)
        + [pl.BlockSpec(memory_space=pl.ANY)] * 2,
        out_specs=(IN_VMEM, IN_VMEM),
        out_shape=(
            pltpu.VMEM((families * order, columns), F32),
            pltpu.VMEM((share * order, columns), F32),
        ),
        scratch_shapes=[
            pltpu.VMEM((len(held) * share_rows, columns), own_half.dtype),
            pltpu.VMEM((share, order, order), own_block.dtype),
            pltpu.VMEM((share_rows, columns), right_side.dtype),
            pltpu.SemaphoreType.DMA((2,)),
        ],
        compiler_params=params(),
        cost_estimate=cost(),
        name="pedigree",
    )(
        rel_family,
        rel_count,
        places,
        *held,
        rel_block,
        solution_part,
        pltpu.with_memory_space_constraint(own_block, pltpu.HBM),
        pltpu.with_memory_space_constraint(right_side, pltpu.HBM),
    )


def chosen(flags, arrays):
    result = None
    for flag, array in zip(flags, arrays):
        if array is None:
            continue
        result = array if result is None else jnp.where(flag, array, result)
    return result


def per_device(
    genotypes,
    allele_frequency,
    family_size,
    rel_family,
    rel_count,
    own_block,
    rel_block,
    prior_solution,
    right_side,
    step_scale,
):
    families, order, _ = own_block.shape
    rows, columns = prior_solution.shape
    words = genotypes.shape[1]
    animals = lax.axis_size("animal")
    snps = lax.axis_size("snp")
    device = lax.axis_index("animal")
    slot = lax.axis_index("snp")
    chips = animals // 2
    chip = lax.div(device, 2)
    even = lax.rem(device, 2) == 0
    distance = jnp.where(even, chip, chips - 1 - chip)
    at_distance = [distance == d for d in range(chips)]
    chunks = CHUNKS
    per_chain = chunks // CHAINS
    width = words // chunks
    markers = width * CODES_PER_WORD
    weight = GEN_WEIGHT / (words * CODES_PER_WORD * snps)
    share = families // snps
    share_rows = share * order

    swap = [(i, i ^ 1) for i in range(animals)]
    along = [(i, i + 2) for i in range(0, animals - 2, 2)] + [(animals - 2, animals - 1)]
    along += [(i, i - 2) for i in range(3, animals, 2)] + [(1, 0)]
    places = jnp.stack([*(slot ^ k for k in range(snps)), device]).astype(jnp.int32)
    row_first = (slot * share_rows).astype(jnp.uint32)
    family_first = (slot * share).astype(jnp.uint32)
    zero = jnp.uint32(0)
    even, at_distance, places, row_first, family_first, prior_solution = lax.optimization_barrier(
        (even, at_distance, places, row_first, family_first, prior_solution)
    )
    frequency = allele_frequency.reshape(1, -1)
    half, sums, centre, first_words = begin(
        genotypes, frequency, family_size, prior_solution, width
    )
    own_half = lax.dynamic_slice(half, (row_first, zero), (share_rows, columns))
    solution_part = own_half.astype(F32)

    codes = [None] * chunks
    fetched = [first_words]
    for iteration in range(ITERS):
        steps = Order()
        sibling = lax.ppermute(own_half, "animal", swap)
        if iteration > 0:
            *shares, sibling = lax.optimization_barrier((*shares, sibling))
            half, sums = join_half(shares, places)
        steps.done(half)

        sent, got, total = [None] * chunks, [None] * chunks, [None] * chunks
        running = rest = None

        def pick(c):
            return c if iteration % 2 == 0 else chunks - 1 - c

        def first_product(c):
            nonlocal fetched
            if iteration == 0:
                codes[c], sent[c], *fetched = decode_and_sum(
                    genotypes, fetched[0], steps.after(half), sums, centre, c, chunks
                )
            else:
                sent[c] = sum_again(codes[pick(c)], steps.after(half), sums, centre, pick(c))
            steps.done(sent[c])
            got[c] = lax.ppermute(sent[c], "animal", swap)

        def chip_sum(c):
            total[c] = steps.done(
                (sent[c].astype(F32) + steps.after(got[c]).astype(F32)).astype(BF16)
            )

        received = [[] for _ in range(CHAINS)]
        passed, other = [None] * chunks, [None] * chunks
        waiting = []

        def chunk_of(c):
            arrived = steps.after(other[c])
            return codes[pick(c)], total[c], passed[c], arrived, centre, pick(c), weight, running

        def second_product():
            nonlocal running
            running = steps.done(add_genomic(*chunk_of(waiting.pop(0))))

        for c in range(CHAINS):
            first_product(c)
        ready = CHAINS
        slots = per_chain + chips - 2
        for j in range(slots + 1):
            for chain in range(CHAINS):
                if j < per_chain:
                    chip_sum(j * CHAINS + chain)
                arrived = None
                if j > 0:
                    arrived = steps.after(received[chain][j - 1])
                    riders = arrived[markers:]
                    arrived = arrived[:markers]
                    received[chain][j - 1] = arrived
                if j < slots:
                    options = [
                        total[(j - d) * CHAINS + chain] if 0 <= j - d < per_chain else None
                        for d in range(chips - 1)
                    ]
                    out = chosen(at_distance, options)
                    if arrived is not None:
                        both = (out.astype(F32) + arrived.astype(F32)).astype(BF16)
                        out = steps.done(jnp.where(at_distance[0], out, both))
                    if chain == 0 and j < 2:
                        out = lax.optimization_barrier((out, out))[0]
                        rider = [own_half, sibling] if j == 0 else [riders[share_rows:]]
                        out = steps.done(jnp.concatenate([out, *rider], axis=0))
                    received[chain].append(lax.ppermute(out, "animal", along))
                if chain == 0 and j == 1:
                    below = riders
                    across = lax.ppermute(below, "animal", swap)
                k = j - (chips - 1)
                if k >= 0:
                    c = k * CHAINS + chain
                    options = [received[chain][k + max(d - 1, 0)] for d in range(chips)]
                    options = steps.after(*options)
                    nothing = jnp.zeros_like(options[0])
                    passed[c] = steps.done(chosen(at_distance, [nothing, *options[1:]]))
                    other[c] = lax.ppermute(passed[c], "animal", swap)
                    waiting.append(c)
                if ready < chunks:
                    first_product(ready)
                    ready += 1
                if chain == 0 and j == 2:
                    across = steps.after(across)
                    first, second = below[share_rows:], below[:share_rows]
                    held = [
                        own_half,
                        jnp.where(even, first, sibling),
                        jnp.where(even, second, across[share_rows:]),
                        jnp.where(even, riders, across[:share_rows]),
                    ]
                    held[1] = steps.after(held[1])
                    running, rest = pedigree(
                        held, rel_family, rel_count, places, rel_block, own_block, right_side, solution_part
                    )
                    steps.done(running)
                if len(waiting) > 1:
                    second_product()
        while len(waiting) > 1:
            second_product()
        parts, *there = last_genomic(*chunk_of(waiting.pop(0)), rest, places)
        others = [
            lax.ppermute(there[k - 1], "snp", [(i, i ^ k) for i in range(snps)])
            for k in range(snps - 1, 0, -1)
        ]
        last = iteration + 1 == ITERS
        sizes, scales, _ = lax.optimization_barrier((family_size, step_scale, parts))
        sizes = lax.dynamic_slice(sizes, (family_first,), (share,))
        live_part = (jnp.arange(order, dtype=jnp.int32)[None, :] < sizes[:, None]).reshape(-1, 1)
        scale_part = lax.dynamic_slice(scales, (row_first,), (share_rows,))[:, None]
        for part in others:
            parts = parts - part.astype(F32)
        residual = jnp.where(live_part, parts, 0.0)
        solution_part = solution_part + scale_part * residual
        result = residual if last else solution_part.astype(BF16)
        if not last:
            own_half = result
            shares = [own_half] + [
                lax.ppermute(own_half, "snp", [(i, i ^ k) for i in range(snps)])
                for k in range(1, snps)
            ]
    return solution_part, result


def solution(mesh):
    in_specs = (
        P("animal", "snp"),
        P("snp"),
        P("animal"),
        P("animal"),
        P("animal"),
        P("animal", None, None),
        P("animal", None, None),
        P("animal", None),
        P("animal", None),
        P("animal"),
    )
    out_specs = (P(("animal", "snp"), None), P(("animal", "snp"), None))
    return jax.shard_map(
        per_device, mesh=mesh, in_specs=in_specs, out_specs=out_specs, check_vma=False
    )
```

```python
import jax
import jax.numpy as jnp
from jax import lax
from jax.experimental import pallas as pl
from jax.experimental.pallas import tpu as pltpu
from jax.sharding import PartitionSpec as P

ITERS = 2
RSPAN = 3
GEN_WEIGHT = 6.0
CODES_PER_WORD = 6
CHUNKS = 8
CHAINS = 2
LANES = 128
PIECE_ROWS = 16
FETCHES = 1
STORES = 2
ROW_BANDS = 8

F8 = jnp.float8_e5m2
BF16 = jnp.bfloat16
F32 = jnp.float32
KERNEL_VMEM = 10 << 20

IN_VMEM = pl.BlockSpec(memory_space=pltpu.VMEM)
IN_SMEM = pl.BlockSpec(memory_space=pltpu.SMEM)


def in_vmem(array):
    return pltpu.with_memory_space_constraint(array, pltpu.VMEM)


def params():
    return pltpu.CompilerParams(vmem_limit_bytes=KERNEL_VMEM)


def cost():
    return pl.CostEstimate(flops=0, bytes_accessed=0, transcendentals=0)


def dot(a, b, a_dim, b_dim):
    return lax.dot_general(a, b, (((a_dim,), (b_dim,)), ((), ())), preferred_element_type=F32)


def pieces(x):
    first = x.astype(BF16)
    left = x - first.astype(F32)
    second = left.astype(BF16)
    third = (left - second.astype(F32)).astype(BF16)
    return first, second, third


class Order:
    def __init__(self):
        self.last = None

    def after(self, *arrays):
        if self.last is None:
            return arrays if len(arrays) > 1 else arrays[0]
        held = lax.optimization_barrier((*arrays, self.last))[:-1]
        return held if len(arrays) > 1 else held[0]

    def done(self, array):
        self.last = array
        return array


def fetch_words(all_ref, words_ref, arrived, chunk):
    rows, width = words_ref.shape
    band = rows // FETCHES
    return [
        pltpu.make_async_copy(
            all_ref.at[pl.ds(i * band, band), pl.ds(chunk * width, width)],
            words_ref.at[pl.ds(i * band, band), :],
            arrived.at[i],
        )
        for i in range(FETCHES)
    ]


def sum_rows(half):
    a, b, c = pieces(jnp.sum(half.astype(F32), axis=0, keepdims=True))
    none = jnp.zeros((PIECE_ROWS - 6, half.shape[1]), BF16)
    return jnp.concatenate([a, b, c, a, b, a, none], axis=0)


def begin(genotypes, frequency, family_size, prior, own_block, right_side, places, width, share):
    rows, columns = prior.shape
    families = family_size.shape[0]
    order = rows // families
    words = genotypes.shape[1]
    lines = words // LANES
    per_chunk = width // LANES
    span = CODES_PER_WORD * LANES

    def body(
        all_ref,
        freq_all,
        size_ref,
        places_ref,
        prior_all,
        own_all,
        right_all,
        half_ref,
        sums_ref,
        centre_ref,
        words_ref,
        own_ref,
        right_ref,
        freq_ref,
        prior_ref,
        arrived,
        others_arrived,
    ):
        freq_fetch = pltpu.make_async_copy(freq_all, freq_ref, others_arrived.at[0])
        freq_fetch.start()
        prior_fetch = pltpu.make_async_copy(prior_all, prior_ref, others_arrived.at[1])
        prior_fetch.start()
        family = places_ref[0] * share
        first = pl.multiple_of(places_ref[0] * (share * order), share * order)
        fetches = fetch_words(all_ref, words_ref, arrived, 0)
        fetches += [
            pltpu.make_async_copy(own_all.at[pl.ds(family, share)], own_ref, others_arrived.at[2]),
            pltpu.make_async_copy(
                right_all.at[pl.ds(first, share * order), :], right_ref, others_arrived.at[3]
            ),
        ]
        for fetch in fetches:
            fetch.start()
        freq_fetch.wait()

        lined = [
            jnp.broadcast_to(freq_ref[:, i * span : (i + 1) * span], (PIECE_ROWS, span)) for i in range(lines)
        ]
        a, b, c = pieces(-2.0 * jnp.concatenate(lined, axis=0))
        which = lax.broadcasted_iota(jnp.int32, (lines * PIECE_ROWS, span), 0) % PIECE_ROWS
        picked = jnp.where(
            which < 3,
            a.astype(F32),
            jnp.where(which < 5, b.astype(F32), jnp.where(which < 6, c.astype(F32), 0.0)),
        ).astype(BF16)
        source = lax.broadcasted_iota(jnp.int32, (span, LANES), 0)
        lane = lax.broadcasted_iota(jnp.int32, (span, LANES), 1)
        code_of = source - CODES_PER_WORD * lane
        for k in range(CODES_PER_WORD):
            place = jnp.where(code_of == k, 1.0, 0.0).astype(BF16)
            moved = dot(picked, place, 1, 0).astype(BF16)
            for line in range(lines):
                chunk, inner = divmod(line, per_chunk)
                at = (chunk * CODES_PER_WORD + k) * width + inner * LANES
                centre_ref[:, at : at + LANES] = moved[line * PIECE_ROWS : (line + 1) * PIECE_ROWS, :]
        prior_fetch.wait()
        row = lax.broadcasted_iota(jnp.int32, (order, columns), 0)
        for f in range(families):
            part = slice(f * order, (f + 1) * order)
            block = prior_ref[part, :]
            half_ref[part, :] = jnp.where(row < size_ref[f], block, jnp.zeros_like(block))
        sums_ref[...] = sum_rows(half_ref[...])
        for fetch in fetches:
            fetch.wait()

    return pl.pallas_call(
        body,
        in_specs=[pl.BlockSpec(memory_space=pl.ANY)] * 2
        + [IN_SMEM] * 2
        + [pl.BlockSpec(memory_space=pl.ANY)] * 3,
        out_specs=[IN_VMEM] * 6,
        out_shape=[
            pltpu.VMEM((rows, columns), BF16),
            pltpu.VMEM((PIECE_ROWS, columns), BF16),
            pltpu.VMEM((PIECE_ROWS, words * CODES_PER_WORD), BF16),
            pltpu.VMEM((rows, width), genotypes.dtype),
            pltpu.VMEM((share, order, order), own_block.dtype),
            pltpu.VMEM((share * order, columns), right_side.dtype),
        ],
        scratch_shapes=[
            pltpu.VMEM(frequency.shape, frequency.dtype),
            pltpu.VMEM((rows, columns), prior.dtype),
            pltpu.SemaphoreType.DMA((FETCHES,)),
            pltpu.SemaphoreType.DMA((4,)),
        ],
        compiler_params=params(),
        cost_estimate=cost(),
        name="begin",
    )(
        pltpu.with_memory_space_constraint(genotypes, pltpu.HBM),
        pltpu.with_memory_space_constraint(frequency, pltpu.HBM),
        family_size,
        places,
        *(pltpu.with_memory_space_constraint(x, pltpu.HBM) for x in (prior, own_block, right_side)),
    )


def join_half(shares, slot):
    count = len(shares)
    share_rows, columns = shares[0].shape
    rows = count * share_rows

    def body(slot_ref, *refs):
        ins, (half_ref, sums_ref) = refs[:count], refs[count:]
        for k in range(count):
            at = pl.multiple_of(slot_ref[k] * share_rows, share_rows)
            half_ref[pl.ds(at, share_rows), :] = ins[k][...]
        sums_ref[...] = sum_rows(half_ref[...])

    return pl.pallas_call(
        body,
        in_specs=[IN_SMEM] + [IN_VMEM] * count,
        out_specs=[IN_VMEM] * 2,
        out_shape=[pltpu.VMEM((rows, columns), BF16), pltpu.VMEM((PIECE_ROWS, columns), BF16)],
        compiler_params=params(),
        cost_estimate=cost(),
        name="join_half",
    )(slot, *shares)


def marker_sums(codes, half, sums, centre, k):
    return (dot(codes, half, 0, 0) * 4.0**-k + dot(centre, sums, 0, 0)).astype(BF16)


def decode_and_sum(genotypes, words, half, sums, centre, chunk, chunks):
    rows, width = words.shape
    columns = half.shape[1]
    markers = CODES_PER_WORD * width
    more = chunk + 1 < chunks
    group = CODES_PER_WORD // STORES

    def body(all_ref, words_ref, half_ref, sums_ref, centre_ref, kept_ref, out_ref, *rest):
        *rest, codes_ref, stored = rest
        copies = fetch_words(all_ref, *rest, chunk + 1) if more else []
        for copy in copies:
            copy.start()
        for k in range(CODES_PER_WORD):
            here = slice(k * width, (k + 1) * width)
            codes_ref[:, here] = jnp.bitwise_and(words_ref[...], 3 << (2 * k)).astype(F32).astype(F8)
            out_ref[here, :] = marker_sums(
                codes_ref[:, here].astype(BF16),
                half_ref[...],
                sums_ref[...],
                centre_ref[:, chunk * markers + k * width : chunk * markers + (k + 1) * width],
                k,
            )
            if (k + 1) % group == 0:
                part = pl.ds((k + 1 - group) * width, group * width)
                copy = pltpu.make_async_copy(
                    codes_ref.at[:, part], kept_ref.at[:, part], stored.at[k // group]
                )
                copy.start()
                copies.append(copy)
        for copy in copies:
            copy.wait()

    out_shape = [pltpu.HBM((rows, markers), F8), pltpu.VMEM((markers, columns), BF16)]
    scratch = [pltpu.VMEM((rows, markers), F8), pltpu.SemaphoreType.DMA((STORES,))]
    if more:
        out_shape.append(pltpu.VMEM((rows, width), words.dtype))
        scratch = [pltpu.SemaphoreType.DMA((FETCHES,)), *scratch]
    return pl.pallas_call(
        body,
        in_specs=[pl.BlockSpec(memory_space=pl.ANY)] + [IN_VMEM] * 4,
        out_specs=[pl.BlockSpec(memory_space=pl.ANY)] + [IN_VMEM] * (len(out_shape) - 1),
        out_shape=out_shape,
        scratch_shapes=scratch,
        compiler_params=params(),
        cost_estimate=cost(),
        name="decode_and_sum",
    )(
        pltpu.with_memory_space_constraint(genotypes, pltpu.HBM),
        *map(in_vmem, (words, half, sums, centre)),
    )


def sum_again(codes, half, sums, centre, chunk):
    rows, markers = codes.shape
    columns = half.shape[1]
    width = markers // CODES_PER_WORD

    def body(codes_ref, half_ref, sums_ref, centre_ref, out_ref):
        for k in range(CODES_PER_WORD):
            here = slice(k * width, (k + 1) * width)
            out_ref[here, :] = marker_sums(
                codes_ref[:, here].astype(BF16),
                half_ref[...],
                sums_ref[...],
                centre_ref[:, chunk * markers + k * width : chunk * markers + (k + 1) * width],
                k,
            )

    return pl.pallas_call(
        body,
        in_specs=[IN_VMEM] * 4,
        out_specs=IN_VMEM,
        out_shape=pltpu.VMEM((markers, columns), BF16),
        compiler_params=params(),
        cost_estimate=cost(),
        name="sum_again",
    )(*map(in_vmem, (codes, half, sums, centre)))


def genomic_steps(codes_ref, own_ref, passed_ref, other_ref, centre_ref, chunk, weight):
    rows, markers = codes_ref.shape
    total = own_ref[...].astype(F32) + passed_ref[...].astype(F32) + other_ref[...].astype(F32)
    total = total.astype(BF16)
    centre = dot(centre_ref[:, chunk * markers : (chunk + 1) * markers], total, 1, 0)
    shift = centre[0:1, :] + centre[3:4, :] + centre[5:6, :]
    width = markers // CODES_PER_WORD
    scaled = jnp.concatenate(
        [total[k * width : (k + 1) * width, :] * BF16(4.0**-k) for k in range(CODES_PER_WORD)]
    )
    band = rows // ROW_BANDS
    for b in range(ROW_BANDS):
        here = slice(b * band, (b + 1) * band)
        yield here, (dot(codes_ref[here, :].astype(BF16), scaled, 1, 0) + shift) * weight


def add_genomic(codes, own, passed, other, centre, chunk, weight, running):
    rows, columns = running.shape

    def body(codes_ref, own_ref, passed_ref, other_ref, centre_ref, run_ref, out_ref):
        for here, step in genomic_steps(
            codes_ref, own_ref, passed_ref, other_ref, centre_ref, chunk, weight
        ):
            out_ref[here, :] = run_ref[here, :] + step

    return pl.pallas_call(
        body,
        in_specs=[IN_VMEM] * 6,
        out_specs=IN_VMEM,
        out_shape=pltpu.VMEM((rows, columns), F32),
        input_output_aliases={5: 0},
        compiler_params=params(),
        cost_estimate=cost(),
        name="add_genomic",
    )(*map(in_vmem, (codes, own, passed, other, centre, running)))


def last_genomic(codes, own, passed, other, centre, chunk, weight, running, rest, slots):
    rows, columns = running.shape
    share_rows = rest.shape[0]
    count = rows // share_rows

    def body(slot_ref, codes_ref, own_ref, passed_ref, other_ref, centre_ref, run_ref, rest_ref, *refs):
        outs, all_ref = refs[:count], refs[count]
        for here, step in genomic_steps(
            codes_ref, own_ref, passed_ref, other_ref, centre_ref, chunk, weight
        ):
            all_ref[here, :] = run_ref[here, :] + step
        for k in range(count):
            at = pl.multiple_of(slot_ref[k] * share_rows, share_rows)
            part = all_ref[pl.ds(at, share_rows), :]
            outs[k][...] = rest_ref[...] - part if k == 0 else part.astype(BF16)

    return pl.pallas_call(
        body,
        in_specs=[IN_SMEM] + [IN_VMEM] * 7,
        out_specs=[IN_VMEM] * count,
        out_shape=[
            pltpu.VMEM((share_rows, columns), F32 if k == 0 else BF16) for k in range(count)
        ],
        scratch_shapes=[pltpu.VMEM(running.shape, F32)],
        compiler_params=params(),
        cost_estimate=cost(),
        name="last_genomic",
    )(slots, *map(in_vmem, (codes, own, passed, other, centre, running, rest)))


def pedigree(held, rel_family, rel_count, places, rel_block, own_part, right_part, solution_part):
    families, order, _ = rel_block.shape
    own_half = held[0]
    share_rows, columns = own_half.shape
    share = share_rows // order

    def body(family_ref, count_ref, places_ref, *refs):
        held_refs, refs = refs[: len(held)], refs[len(held) :]
        rel_ref, solution_ref, own_ref, right_ref, out_ref, rest_ref, all_ref = refs
        slot, device = places_ref[0], places_ref[places_ref.shape[0] - 1]
        for d, ref in enumerate(held_refs):
            all_ref[d * share_rows : (d + 1) * share_rows, :] = ref[...]
        row = lax.broadcasted_iota(jnp.int32, (order, columns), 0)
        for f in range(families):
            away = device - lax.div(family_ref[f], families)
            inside = lax.rem(family_ref[f], families)
            at = jnp.clip(away * share + lax.rem(inside, share), 0, len(held) * share - 1)
            count = jnp.where(lax.div(inside, share) == slot, count_ref[f], 0)
            relative = all_ref[pl.ds(pl.multiple_of(at * order, order), order), :]
            relative = jnp.where(row < count, relative, jnp.zeros_like(relative))
            out_ref[f * order : (f + 1) * order, :] = dot(rel_ref[f], relative, 1, 0)
        for f in range(share):
            part = slice(f * order, (f + 1) * order)
            own = dot(own_ref[f], held_refs[0][part, :], 1, 0)
            rest_ref[part, :] = right_ref[part, :] - solution_ref[part, :] - own

    return pl.pallas_call(
        body,
        in_specs=[IN_SMEM] * 3 + [IN_VMEM] * (len(held) + 4),
        out_specs=(IN_VMEM, IN_VMEM),
        out_shape=(
            pltpu.VMEM((families * order, columns), F32),
            pltpu.VMEM((share * order, columns), F32),
        ),
        scratch_shapes=[pltpu.VMEM((len(held) * share_rows, columns), own_half.dtype)],
        compiler_params=params(),
        cost_estimate=cost(),
        name="pedigree",
    )(
        rel_family,
        rel_count,
        places,
        *held,
        rel_block,
        solution_part,
        *map(in_vmem, (own_part, right_part)),
    )


def chosen(flags, arrays):
    result = None
    for flag, array in zip(flags, arrays):
        if array is None:
            continue
        result = array if result is None else jnp.where(flag, array, result)
    return result


def per_device(
    genotypes,
    allele_frequency,
    family_size,
    rel_family,
    rel_count,
    own_block,
    rel_block,
    prior_solution,
    right_side,
    step_scale,
):
    families, order, _ = own_block.shape
    rows, columns = prior_solution.shape
    words = genotypes.shape[1]
    animals = lax.axis_size("animal")
    snps = lax.axis_size("snp")
    device = lax.axis_index("animal")
    slot = lax.axis_index("snp")
    chips = animals // 2
    chip = lax.div(device, 2)
    even = lax.rem(device, 2) == 0
    distance = jnp.where(even, chip, chips - 1 - chip)
    at_distance = [distance == d for d in range(chips)]
    chunks = CHUNKS
    per_chain = chunks // CHAINS
    width = words // chunks
    markers = width * CODES_PER_WORD
    weight = GEN_WEIGHT / (words * CODES_PER_WORD * snps)
    share = families // snps
    share_rows = share * order

    swap = [(i, i ^ 1) for i in range(animals)]
    along = [(i, i + 2) for i in range(0, animals - 2, 2)] + [(animals - 2, animals - 1)]
    along += [(i, i - 2) for i in range(3, animals, 2)] + [(1, 0)]
    places = jnp.stack([*(slot ^ k for k in range(snps)), device]).astype(jnp.int32)
    row_first = (slot * share_rows).astype(jnp.uint32)
    family_first = (slot * share).astype(jnp.uint32)
    zero = jnp.uint32(0)
    even, at_distance, places, row_first, family_first, prior_solution = lax.optimization_barrier(
        (even, at_distance, places, row_first, family_first, prior_solution)
    )
    frequency = allele_frequency.reshape(1, -1)
    half, sums, centre, first_words, own_part, right_part = begin(
        genotypes, frequency, family_size, prior_solution, own_block, right_side, places, width, share
    )
    own_half = lax.dynamic_slice(half, (row_first, zero), (share_rows, columns))
    solution_part = own_half.astype(F32)

    codes = [None] * chunks
    fetched = [first_words]
    for iteration in range(ITERS):
        steps = Order()
        sibling = lax.ppermute(own_half, "animal", swap)
        if iteration > 0:
            *shares, sibling = lax.optimization_barrier((*shares, sibling))
            half, sums = join_half(shares, places)
        steps.done(half)

        sent, got, total = [None] * chunks, [None] * chunks, [None] * chunks
        running = rest = None

        def pick(c):
            return c if iteration % 2 == 0 else chunks - 1 - c

        def first_product(c):
            nonlocal fetched
            if iteration == 0:
                codes[c], sent[c], *fetched = decode_and_sum(
                    genotypes, fetched[0], steps.after(half), sums, centre, c, chunks
                )
            else:
                sent[c] = sum_again(codes[pick(c)], steps.after(half), sums, centre, pick(c))
            steps.done(sent[c])
            got[c] = lax.ppermute(sent[c], "animal", swap)

        def chip_sum(c):
            total[c] = steps.done(
                (sent[c].astype(F32) + steps.after(got[c]).astype(F32)).astype(BF16)
            )

        received = [[] for _ in range(CHAINS)]
        passed, other = [None] * chunks, [None] * chunks
        waiting = []

        def chunk_of(c):
            arrived = steps.after(other[c])
            return codes[pick(c)], total[c], passed[c], arrived, centre, pick(c), weight, running

        def second_product():
            nonlocal running
            running = steps.done(add_genomic(*chunk_of(waiting.pop(0))))

        for c in range(CHAINS):
            first_product(c)
        ready = CHAINS
        slots = per_chain + chips - 2
        for j in range(slots + 1):
            for chain in range(CHAINS):
                if j < per_chain:
                    chip_sum(j * CHAINS + chain)
                arrived = None
                if j > 0:
                    arrived = steps.after(received[chain][j - 1])
                    riders = arrived[markers:]
                    arrived = arrived[:markers]
                    received[chain][j - 1] = arrived
                if j < slots:
                    options = [
                        total[(j - d) * CHAINS + chain] if 0 <= j - d < per_chain else None
                        for d in range(chips - 1)
                    ]
                    out = chosen(at_distance, options)
                    if arrived is not None:
                        both = (out.astype(F32) + arrived.astype(F32)).astype(BF16)
                        out = steps.done(jnp.where(at_distance[0], out, both))
                    if chain == 0 and j < 2:
                        out = lax.optimization_barrier((out, out))[0]
                        rider = [own_half, sibling] if j == 0 else [riders[share_rows:]]
                        out = steps.done(jnp.concatenate([out, *rider], axis=0))
                    received[chain].append(lax.ppermute(out, "animal", along))
                if chain == 0 and j == 1:
                    below = riders
                    across = lax.ppermute(below, "animal", swap)
                k = j - (chips - 1)
                if k >= 0:
                    c = k * CHAINS + chain
                    options = [received[chain][k + max(d - 1, 0)] for d in range(chips)]
                    options = steps.after(*options)
                    nothing = jnp.zeros_like(options[0])
                    passed[c] = steps.done(chosen(at_distance, [nothing, *options[1:]]))
                    other[c] = lax.ppermute(passed[c], "animal", swap)
                    waiting.append(c)
                if ready < chunks:
                    first_product(ready)
                    ready += 1
                if chain == 0 and j == 2:
                    across = steps.after(across)
                    first, second = below[share_rows:], below[:share_rows]
                    held = [
                        own_half,
                        jnp.where(even, first, sibling),
                        jnp.where(even, second, across[share_rows:]),
                        jnp.where(even, riders, across[:share_rows]),
                    ]
                    held[1] = steps.after(held[1])
                    running, rest = pedigree(
                        held, rel_family, rel_count, places, rel_block, own_part, right_part, solution_part
                    )
                    steps.done(running)
                if len(waiting) > 1:
                    second_product()
        while len(waiting) > 1:
            second_product()
        parts, *there = last_genomic(*chunk_of(waiting.pop(0)), rest, places)
        others = [
            lax.ppermute(there[k - 1], "snp", [(i, i ^ k) for i in range(snps)])
            for k in range(snps - 1, 0, -1)
        ]
        last = iteration + 1 == ITERS
        sizes, scales, _ = lax.optimization_barrier((family_size, step_scale, parts))
        sizes = lax.dynamic_slice(sizes, (family_first,), (share,))
        live_part = (jnp.arange(order, dtype=jnp.int32)[None, :] < sizes[:, None]).reshape(-1, 1)
        scale_part = lax.dynamic_slice(scales, (row_first,), (share_rows,))[:, None]
        for part in others:
            parts = parts - part.astype(F32)
        residual = jnp.where(live_part, parts, 0.0)
        solution_part = solution_part + scale_part * residual
        result = residual if last else solution_part.astype(BF16)
        if not last:
            own_half = result
            shares = [own_half] + [
                lax.ppermute(own_half, "snp", [(i, i ^ k) for i in range(snps)])
                for k in range(1, snps)
            ]
    return solution_part, result


def solution(mesh):
    in_specs = (
        P("animal", "snp"),
        P("snp"),
        P("animal"),
        P("animal"),
        P("animal"),
        P("animal", None, None),
        P("animal", None, None),
        P("animal", None),
        P("animal", None),
        P("animal"),
    )
    out_specs = (P(("animal", "snp"), None), P(("animal", "snp"), None))
    return jax.shard_map(
        per_device, mesh=mesh, in_specs=in_specs, out_specs=out_specs, check_vma=False
    )
```

```python
import jax
import jax.numpy as jnp
from jax import lax
from jax.experimental import pallas as pl
from jax.experimental.pallas import tpu as pltpu
from jax.sharding import PartitionSpec as P

ITERS = 2
RSPAN = 3
GEN_WEIGHT = 6.0
CODES_PER_WORD = 6
CHUNKS = 8
CHAINS = 2
LANES = 128
PIECE_ROWS = 16
FETCHES = 1
STORES = 3
ROW_BANDS = 8

F8 = jnp.float8_e5m2
BF16 = jnp.bfloat16
F32 = jnp.float32
KERNEL_VMEM = 10 << 20

IN_VMEM = pl.BlockSpec(memory_space=pltpu.VMEM)
IN_SMEM = pl.BlockSpec(memory_space=pltpu.SMEM)


def in_vmem(array):
    return pltpu.with_memory_space_constraint(array, pltpu.VMEM)


def params():
    return pltpu.CompilerParams(vmem_limit_bytes=KERNEL_VMEM)


def cost():
    return pl.CostEstimate(flops=0, bytes_accessed=0, transcendentals=0)


def dot(a, b, a_dim, b_dim):
    return lax.dot_general(a, b, (((a_dim,), (b_dim,)), ((), ())), preferred_element_type=F32)


def pieces(x):
    first = x.astype(BF16)
    left = x - first.astype(F32)
    second = left.astype(BF16)
    third = (left - second.astype(F32)).astype(BF16)
    return first, second, third


class Order:
    def __init__(self):
        self.last = None

    def after(self, *arrays):
        if self.last is None:
            return arrays if len(arrays) > 1 else arrays[0]
        held = lax.optimization_barrier((*arrays, self.last))[:-1]
        return held if len(arrays) > 1 else held[0]

    def done(self, array):
        self.last = array
        return array


def fetch_words(all_ref, words_ref, arrived, chunk):
    rows, width = words_ref.shape
    band = rows // FETCHES
    return [
        pltpu.make_async_copy(
            all_ref.at[pl.ds(i * band, band), pl.ds(chunk * width, width)],
            words_ref.at[pl.ds(i * band, band), :],
            arrived.at[i],
        )
        for i in range(FETCHES)
    ]


def sum_rows(half):
    a, b, c = pieces(jnp.sum(half.astype(F32), axis=0, keepdims=True))
    none = jnp.zeros((PIECE_ROWS - 6, half.shape[1]), BF16)
    return jnp.concatenate([a, b, c, a, b, a, none], axis=0)


def begin(genotypes, frequency, family_size, prior, own_block, right_side, places, width, share):
    rows, columns = prior.shape
    families = family_size.shape[0]
    order = rows // families
    words = genotypes.shape[1]
    lines = words // LANES
    per_chunk = width // LANES
    span = CODES_PER_WORD * LANES

    def body(
        all_ref,
        freq_all,
        size_ref,
        places_ref,
        prior_all,
        own_all,
        right_all,
        half_ref,
        sums_ref,
        centre_ref,
        words_ref,
        own_ref,
        right_ref,
        freq_ref,
        prior_ref,
        arrived,
        others_arrived,
    ):
        freq_fetch = pltpu.make_async_copy(freq_all, freq_ref, others_arrived.at[0])
        freq_fetch.start()
        prior_fetch = pltpu.make_async_copy(prior_all, prior_ref, others_arrived.at[1])
        prior_fetch.start()
        family = places_ref[0] * share
        first = pl.multiple_of(places_ref[0] * (share * order), share * order)
        fetches = fetch_words(all_ref, words_ref, arrived, 0)
        fetches += [
            pltpu.make_async_copy(own_all.at[pl.ds(family, share)], own_ref, others_arrived.at[2]),
            pltpu.make_async_copy(
                right_all.at[pl.ds(first, share * order), :], right_ref, others_arrived.at[3]
            ),
        ]
        for fetch in fetches:
            fetch.start()
        freq_fetch.wait()

        lined = [
            jnp.broadcast_to(freq_ref[:, i * span : (i + 1) * span], (PIECE_ROWS, span)) for i in range(lines)
        ]
        a, b, c = pieces(-2.0 * jnp.concatenate(lined, axis=0))
        which = lax.broadcasted_iota(jnp.int32, (lines * PIECE_ROWS, span), 0) % PIECE_ROWS
        picked = jnp.where(
            which < 3,
            a.astype(F32),
            jnp.where(which < 5, b.astype(F32), jnp.where(which < 6, c.astype(F32), 0.0)),
        ).astype(BF16)
        source = lax.broadcasted_iota(jnp.int32, (span, LANES), 0)
        lane = lax.broadcasted_iota(jnp.int32, (span, LANES), 1)
        code_of = source - CODES_PER_WORD * lane
        for k in range(CODES_PER_WORD):
            place = jnp.where(code_of == k, 1.0, 0.0).astype(BF16)
            moved = dot(picked, place, 1, 0).astype(BF16)
            for line in range(lines):
                chunk, inner = divmod(line, per_chunk)
                at = (chunk * CODES_PER_WORD + k) * width + inner * LANES
                centre_ref[:, at : at + LANES] = moved[line * PIECE_ROWS : (line + 1) * PIECE_ROWS, :]
        prior_fetch.wait()
        row = lax.broadcasted_iota(jnp.int32, (order, columns), 0)
        for f in range(families):
            part = slice(f * order, (f + 1) * order)
            block = prior_ref[part, :]
            half_ref[part, :] = jnp.where(row < size_ref[f], block, jnp.zeros_like(block))
        sums_ref[...] = sum_rows(half_ref[...])
        for fetch in fetches:
            fetch.wait()

    return pl.pallas_call(
        body,
        in_specs=[pl.BlockSpec(memory_space=pl.ANY)] * 2
        + [IN_SMEM] * 2
        + [pl.BlockSpec(memory_space=pl.ANY)] * 3,
        out_specs=[IN_VMEM] * 6,
        out_shape=[
            pltpu.VMEM((rows, columns), BF16),
            pltpu.VMEM((PIECE_ROWS, columns), BF16),
            pltpu.VMEM((PIECE_ROWS, words * CODES_PER_WORD), BF16),
            pltpu.VMEM((rows, width), genotypes.dtype),
            pltpu.VMEM((share, order, order), own_block.dtype),
            pltpu.VMEM((share * order, columns), right_side.dtype),
        ],
        scratch_shapes=[
            pltpu.VMEM(frequency.shape, frequency.dtype),
            pltpu.VMEM((rows, columns), prior.dtype),
            pltpu.SemaphoreType.DMA((FETCHES,)),
            pltpu.SemaphoreType.DMA((4,)),
        ],
        compiler_params=params(),
        cost_estimate=cost(),
        name="begin",
    )(
        pltpu.with_memory_space_constraint(genotypes, pltpu.HBM),
        pltpu.with_memory_space_constraint(frequency, pltpu.HBM),
        family_size,
        places,
        *(pltpu.with_memory_space_constraint(x, pltpu.HBM) for x in (prior, own_block, right_side)),
    )


def join_half(shares, slot):
    count = len(shares)
    share_rows, columns = shares[0].shape
    rows = count * share_rows

    def body(slot_ref, *refs):
        ins, (half_ref, sums_ref) = refs[:count], refs[count:]
        for k in range(count):
            at = pl.multiple_of(slot_ref[k] * share_rows, share_rows)
            half_ref[pl.ds(at, share_rows), :] = ins[k][...]
        sums_ref[...] = sum_rows(half_ref[...])

    return pl.pallas_call(
        body,
        in_specs=[IN_SMEM] + [IN_VMEM] * count,
        out_specs=[IN_VMEM] * 2,
        out_shape=[pltpu.VMEM((rows, columns), BF16), pltpu.VMEM((PIECE_ROWS, columns), BF16)],
        compiler_params=params(),
        cost_estimate=cost(),
        name="join_half",
    )(slot, *shares)


def marker_sums(codes, half, sums, centre, k):
    return (dot(codes, half, 0, 0) * 4.0**-k + dot(centre, sums, 0, 0)).astype(BF16)


def decode_and_sum(genotypes, words, half, sums, centre, chunk, chunks):
    rows, width = words.shape
    columns = half.shape[1]
    markers = CODES_PER_WORD * width
    more = chunk + 1 < chunks
    group = CODES_PER_WORD // STORES

    def body(all_ref, words_ref, half_ref, sums_ref, centre_ref, kept_ref, out_ref, *rest):
        *rest, codes_ref, stored = rest
        copies = fetch_words(all_ref, *rest, chunk + 1) if more else []
        for copy in copies:
            copy.start()
        for k in range(CODES_PER_WORD):
            here = slice(k * width, (k + 1) * width)
            codes_ref[:, here] = jnp.bitwise_and(words_ref[...], 3 << (2 * k)).astype(F32).astype(F8)
            out_ref[here, :] = marker_sums(
                codes_ref[:, here].astype(BF16),
                half_ref[...],
                sums_ref[...],
                centre_ref[:, chunk * markers + k * width : chunk * markers + (k + 1) * width],
                k,
            )
            if (k + 1) % group == 0:
                part = pl.ds((k + 1 - group) * width, group * width)
                copy = pltpu.make_async_copy(
                    codes_ref.at[:, part], kept_ref.at[:, part], stored.at[k // group]
                )
                copy.start()
                copies.append(copy)
        for copy in copies:
            copy.wait()

    out_shape = [pltpu.HBM((rows, markers), F8), pltpu.VMEM((markers, columns), BF16)]
    scratch = [pltpu.VMEM((rows, markers), F8), pltpu.SemaphoreType.DMA((STORES,))]
    if more:
        out_shape.append(pltpu.VMEM((rows, width), words.dtype))
        scratch = [pltpu.SemaphoreType.DMA((FETCHES,)), *scratch]
    return pl.pallas_call(
        body,
        in_specs=[pl.BlockSpec(memory_space=pl.ANY)] + [IN_VMEM] * 4,
        out_specs=[pl.BlockSpec(memory_space=pl.ANY)] + [IN_VMEM] * (len(out_shape) - 1),
        out_shape=out_shape,
        scratch_shapes=scratch,
        compiler_params=params(),
        cost_estimate=cost(),
        name="decode_and_sum",
    )(
        pltpu.with_memory_space_constraint(genotypes, pltpu.HBM),
        *map(in_vmem, (words, half, sums, centre)),
    )


def sum_again(codes, half, sums, centre, chunk):
    rows, markers = codes.shape
    columns = half.shape[1]
    width = markers // CODES_PER_WORD

    def body(codes_ref, half_ref, sums_ref, centre_ref, out_ref):
        for k in range(CODES_PER_WORD):
            here = slice(k * width, (k + 1) * width)
            out_ref[here, :] = marker_sums(
                codes_ref[:, here].astype(BF16),
                half_ref[...],
                sums_ref[...],
                centre_ref[:, chunk * markers + k * width : chunk * markers + (k + 1) * width],
                k,
            )

    return pl.pallas_call(
        body,
        in_specs=[IN_VMEM] * 4,
        out_specs=IN_VMEM,
        out_shape=pltpu.VMEM((markers, columns), BF16),
        compiler_params=params(),
        cost_estimate=cost(),
        name="sum_again",
    )(*map(in_vmem, (codes, half, sums, centre)))


def genomic_steps(codes_ref, own_ref, passed_ref, other_ref, centre_ref, chunk, weight):
    rows, markers = codes_ref.shape
    total = own_ref[...].astype(F32) + passed_ref[...].astype(F32) + other_ref[...].astype(F32)
    total = total.astype(BF16)
    centre = dot(centre_ref[:, chunk * markers : (chunk + 1) * markers], total, 1, 0)
    shift = centre[0:1, :] + centre[3:4, :] + centre[5:6, :]
    width = markers // CODES_PER_WORD
    scaled = jnp.concatenate(
        [total[k * width : (k + 1) * width, :] * BF16(4.0**-k) for k in range(CODES_PER_WORD)]
    )
    band = rows // ROW_BANDS
    for b in range(ROW_BANDS):
        here = slice(b * band, (b + 1) * band)
        yield here, (dot(codes_ref[here, :].astype(BF16), scaled, 1, 0) + shift) * weight


def add_genomic(codes, own, passed, other, centre, chunk, weight, running):
    rows, columns = running.shape

    def body(codes_ref, own_ref, passed_ref, other_ref, centre_ref, run_ref, out_ref):
        for here, step in genomic_steps(
            codes_ref, own_ref, passed_ref, other_ref, centre_ref, chunk, weight
        ):
            out_ref[here, :] = run_ref[here, :] + step

    return pl.pallas_call(
        body,
        in_specs=[IN_VMEM] * 6,
        out_specs=IN_VMEM,
        out_shape=pltpu.VMEM((rows, columns), F32),
        input_output_aliases={5: 0},
        compiler_params=params(),
        cost_estimate=cost(),
        name="add_genomic",
    )(*map(in_vmem, (codes, own, passed, other, centre, running)))


def last_genomic(codes, own, passed, other, centre, chunk, weight, running, rest, slots):
    rows, columns = running.shape
    share_rows = rest.shape[0]
    count = rows // share_rows

    def body(slot_ref, codes_ref, own_ref, passed_ref, other_ref, centre_ref, run_ref, rest_ref, *refs):
        outs, all_ref = refs[:count], refs[count]
        for here, step in genomic_steps(
            codes_ref, own_ref, passed_ref, other_ref, centre_ref, chunk, weight
        ):
            all_ref[here, :] = run_ref[here, :] + step
        for k in range(count):
            at = pl.multiple_of(slot_ref[k] * share_rows, share_rows)
            part = all_ref[pl.ds(at, share_rows), :]
            outs[k][...] = rest_ref[...] - part if k == 0 else part.astype(BF16)

    return pl.pallas_call(
        body,
        in_specs=[IN_SMEM] + [IN_VMEM] * 7,
        out_specs=[IN_VMEM] * count,
        out_shape=[
            pltpu.VMEM((share_rows, columns), F32 if k == 0 else BF16) for k in range(count)
        ],
        scratch_shapes=[pltpu.VMEM(running.shape, F32)],
        compiler_params=params(),
        cost_estimate=cost(),
        name="last_genomic",
    )(slots, *map(in_vmem, (codes, own, passed, other, centre, running, rest)))


def pedigree(held, rel_family, rel_count, places, rel_block, own_part, right_part, solution_part):
    families, order, _ = rel_block.shape
    own_half = held[0]
    share_rows, columns = own_half.shape
    share = share_rows // order

    def body(family_ref, count_ref, places_ref, *refs):
        held_refs, refs = refs[: len(held)], refs[len(held) :]
        rel_ref, solution_ref, own_ref, right_ref, out_ref, rest_ref, all_ref = refs
        slot, device = places_ref[0], places_ref[places_ref.shape[0] - 1]
        for d, ref in enumerate(held_refs):
            all_ref[d * share_rows : (d + 1) * share_rows, :] = ref[...]
        row = lax.broadcasted_iota(jnp.int32, (order, columns), 0)
        for f in range(families):
            away = device - lax.div(family_ref[f], families)
            inside = lax.rem(family_ref[f], families)
            at = jnp.clip(away * share + lax.rem(inside, share), 0, len(held) * share - 1)
            count = jnp.where(lax.div(inside, share) == slot, count_ref[f], 0)
            relative = all_ref[pl.ds(pl.multiple_of(at * order, order), order), :]
            relative = jnp.where(row < count, relative, jnp.zeros_like(relative))
            out_ref[f * order : (f + 1) * order, :] = dot(rel_ref[f], relative, 1, 0)
        for f in range(share):
            part = slice(f * order, (f + 1) * order)
            own = dot(own_ref[f], held_refs[0][part, :], 1, 0)
            rest_ref[part, :] = right_ref[part, :] - solution_ref[part, :] - own

    return pl.pallas_call(
        body,
        in_specs=[IN_SMEM] * 3 + [IN_VMEM] * (len(held) + 4),
        out_specs=(IN_VMEM, IN_VMEM),
        out_shape=(
            pltpu.VMEM((families * order, columns), F32),
            pltpu.VMEM((share * order, columns), F32),
        ),
        scratch_shapes=[pltpu.VMEM((len(held) * share_rows, columns), own_half.dtype)],
        compiler_params=params(),
        cost_estimate=cost(),
        name="pedigree",
    )(
        rel_family,
        rel_count,
        places,
        *held,
        rel_block,
        solution_part,
        *map(in_vmem, (own_part, right_part)),
    )


def chosen(flags, arrays):
    result = None
    for flag, array in zip(flags, arrays):
        if array is None:
            continue
        result = array if result is None else jnp.where(flag, array, result)
    return result


def per_device(
    genotypes,
    allele_frequency,
    family_size,
    rel_family,
    rel_count,
    own_block,
    rel_block,
    prior_solution,
    right_side,
    step_scale,
):
    families, order, _ = own_block.shape
    rows, columns = prior_solution.shape
    words = genotypes.shape[1]
    animals = lax.axis_size("animal")
    snps = lax.axis_size("snp")
    device = lax.axis_index("animal")
    slot = lax.axis_index("snp")
    chips = animals // 2
    chip = lax.div(device, 2)
    even = lax.rem(device, 2) == 0
    distance = jnp.where(even, chip, chips - 1 - chip)
    at_distance = [distance == d for d in range(chips)]
    chunks = CHUNKS
    per_chain = chunks // CHAINS
    width = words // chunks
    markers = width * CODES_PER_WORD
    weight = GEN_WEIGHT / (words * CODES_PER_WORD * snps)
    share = families // snps
    share_rows = share * order

    swap = [(i, i ^ 1) for i in range(animals)]
    along = [(i, i + 2) for i in range(0, animals - 2, 2)] + [(animals - 2, animals - 1)]
    along += [(i, i - 2) for i in range(3, animals, 2)] + [(1, 0)]
    places = jnp.stack([*(slot ^ k for k in range(snps)), device]).astype(jnp.int32)
    row_first = (slot * share_rows).astype(jnp.uint32)
    family_first = (slot * share).astype(jnp.uint32)
    zero = jnp.uint32(0)
    even, at_distance, places, row_first, family_first, prior_solution = lax.optimization_barrier(
        (even, at_distance, places, row_first, family_first, prior_solution)
    )
    frequency = allele_frequency.reshape(1, -1)
    half, sums, centre, first_words, own_part, right_part = begin(
        genotypes, frequency, family_size, prior_solution, own_block, right_side, places, width, share
    )
    own_half = lax.dynamic_slice(half, (row_first, zero), (share_rows, columns))
    solution_part = own_half.astype(F32)

    codes = [None] * chunks
    fetched = [first_words]
    for iteration in range(ITERS):
        steps = Order()
        sibling = lax.ppermute(own_half, "animal", swap)
        if iteration > 0:
            *shares, sibling = lax.optimization_barrier((*shares, sibling))
            half, sums = join_half(shares, places)
        steps.done(half)

        sent, got, total = [None] * chunks, [None] * chunks, [None] * chunks
        running = rest = None

        def pick(c):
            return c if iteration % 2 == 0 else chunks - 1 - c

        def first_product(c):
            nonlocal fetched
            if iteration == 0:
                codes[c], sent[c], *fetched = decode_and_sum(
                    genotypes, fetched[0], steps.after(half), sums, centre, c, chunks
                )
            else:
                sent[c] = sum_again(codes[pick(c)], steps.after(half), sums, centre, pick(c))
            steps.done(sent[c])
            got[c] = lax.ppermute(sent[c], "animal", swap)

        def chip_sum(c):
            total[c] = steps.done(
                (sent[c].astype(F32) + steps.after(got[c]).astype(F32)).astype(BF16)
            )

        received = [[] for _ in range(CHAINS)]
        passed, other = [None] * chunks, [None] * chunks
        waiting = []

        def chunk_of(c):
            arrived = steps.after(other[c])
            return codes[pick(c)], total[c], passed[c], arrived, centre, pick(c), weight, running

        def second_product():
            nonlocal running
            running = steps.done(add_genomic(*chunk_of(waiting.pop(0))))

        for c in range(CHAINS):
            first_product(c)
        ready = CHAINS
        slots = per_chain + chips - 2
        for j in range(slots + 1):
            for chain in range(CHAINS):
                if j < per_chain:
                    chip_sum(j * CHAINS + chain)
                arrived = None
                if j > 0:
                    arrived = steps.after(received[chain][j - 1])
                    riders = arrived[markers:]
                    arrived = arrived[:markers]
                    received[chain][j - 1] = arrived
                if j < slots:
                    options = [
                        total[(j - d) * CHAINS + chain] if 0 <= j - d < per_chain else None
                        for d in range(chips - 1)
                    ]
                    out = chosen(at_distance, options)
                    if arrived is not None:
                        both = (out.astype(F32) + arrived.astype(F32)).astype(BF16)
                        out = steps.done(jnp.where(at_distance[0], out, both))
                    if chain == 0 and j < 2:
                        out = lax.optimization_barrier((out, out))[0]
                        rider = [own_half, sibling] if j == 0 else [riders[share_rows:]]
                        out = steps.done(jnp.concatenate([out, *rider], axis=0))
                    received[chain].append(lax.ppermute(out, "animal", along))
                if chain == 0 and j == 1:
                    below = riders
                    across = lax.ppermute(below, "animal", swap)
                k = j - (chips - 1)
                if k >= 0:
                    c = k * CHAINS + chain
                    options = [received[chain][k + max(d - 1, 0)] for d in range(chips)]
                    options = steps.after(*options)
                    nothing = jnp.zeros_like(options[0])
                    passed[c] = steps.done(chosen(at_distance, [nothing, *options[1:]]))
                    other[c] = lax.ppermute(passed[c], "animal", swap)
                    waiting.append(c)
                if ready < chunks:
                    first_product(ready)
                    ready += 1
                if chain == 0 and j == 2:
                    across = steps.after(across)
                    first, second = below[share_rows:], below[:share_rows]
                    held = [
                        own_half,
                        jnp.where(even, first, sibling),
                        jnp.where(even, second, across[share_rows:]),
                        jnp.where(even, riders, across[:share_rows]),
                    ]
                    held[1] = steps.after(held[1])
                    running, rest = pedigree(
                        held, rel_family, rel_count, places, rel_block, own_part, right_part, solution_part
                    )
                    steps.done(running)
                if len(waiting) > 1:
                    second_product()
        while len(waiting) > 1:
            second_product()
        parts, *there = last_genomic(*chunk_of(waiting.pop(0)), rest, places)
        others = [
            lax.ppermute(there[k - 1], "snp", [(i, i ^ k) for i in range(snps)])
            for k in range(snps - 1, 0, -1)
        ]
        last = iteration + 1 == ITERS
        sizes, scales, _ = lax.optimization_barrier((family_size, step_scale, parts))
        sizes = lax.dynamic_slice(sizes, (family_first,), (share,))
        live_part = (jnp.arange(order, dtype=jnp.int32)[None, :] < sizes[:, None]).reshape(-1, 1)
        scale_part = lax.dynamic_slice(scales, (row_first,), (share_rows,))[:, None]
        for part in others:
            parts = parts - part.astype(F32)
        residual = jnp.where(live_part, parts, 0.0)
        solution_part = solution_part + scale_part * residual
        result = residual if last else solution_part.astype(BF16)
        if not last:
            own_half = result
            shares = [own_half] + [
                lax.ppermute(own_half, "snp", [(i, i ^ k) for i in range(snps)])
                for k in range(1, snps)
            ]
    return solution_part, result


def solution(mesh):
    in_specs = (
        P("animal", "snp"),
        P("snp"),
        P("animal"),
        P("animal"),
        P("animal"),
        P("animal", None, None),
        P("animal", None, None),
        P("animal", None),
        P("animal", None),
        P("animal"),
    )
    out_specs = (P(("animal", "snp"), None), P(("animal", "snp"), None))
    return jax.shard_map(
        per_device, mesh=mesh, in_specs=in_specs, out_specs=out_specs, check_vma=False
    )
```
